512 devices in a mesh: row: 32 (over y, x, z_hi), col: 16 (over z_lo, core).
Axes of the slice: x: 4, y: 4, z: 16 (z_hi: 2, z_lo: 8; z = z_hi * 8 + z_lo), core: 2. Of those that a mesh axis runs over, the one named last changes fastest.
Arguments:
- x_block: float32 [8, 131072], P(None, ('row', 'col')), may hold values from -6 to 6
- p_block: float32 [8, 131072], P(None, ('row', 'col')), may hold values from -6 to 6
- hp_block: float32 [8, 131072], P(None, ('row', 'col')), may hold values from -6 to 6
- tile_rows: int32 [32, 16, 48], P('row', 'col'), may hold values from 0 to 31, as said below
- tile_cols: int32 [32, 16, 48], P('row', 'col'), may hold values from 0 to 63
- tile_count: int32 [32, 16], P('row', 'col'), may hold values from 1 to 48, as said below
- tile_values: bfloat16 [32, 16, 48, 128, 128], P('row', 'col'), may hold values from -0.109375 to 0.109375
Outputs:
- residual: float32 [8, 131072], P(None, ('row', 'col'))
- image: float32 [8, 131072], P(None, ('row', 'col'))
- gram_s: float32 [24, 24], replicated
- gram_h: float32 [24, 24], replicated
The draws below stay inside these ranges and needn't reach their ends.
Inputs may be any that keep to these rules, and one draw needn't show every extreme that they name: `tile_rows`: together with tile_cols, every live tile lies on or below the diagonal of segments. `tile_count`: every device has at least one live slot; some device has all 48 slots live.
All inputs are finite; a program needn't handle non-finite values.
Results may differ from the reference program's by a relative error of at most 0.007.
Values may be sent and summed in bfloat16 or wider, within the bound.
A program may use at most 64 MiB of HBM per device.

```python
import jax
import jax.numpy as jnp
from jax import lax

TILE = 128
VECS = 8
BLK = 2
TILES_DEV = 48
ROWB = 32
NV = 131072
N_ROW = 32
N_COL = 16


def tile_pattern(key):
    shape = (N_ROW, N_COL, TILES_DEV)
    key_group, key_offset, key_row = jax.random.split(key, 3)
    row_ids = jnp.broadcast_to(jnp.arange(N_ROW, dtype=jnp.int32)[:, None, None], shape)
    col_ids = jnp.broadcast_to(jnp.arange(N_COL, dtype=jnp.int32)[None, :, None], shape)
    source_group = jax.random.randint(key_group, shape, 0, row_ids + 1)
    offset = jax.random.randint(key_offset, shape, 0, BLK)
    local_row = jax.random.randint(key_row, shape, 0, ROWB)
    local_row = jnp.where(source_group == row_ids, jnp.maximum(local_row, col_ids * BLK + offset), local_row)
    return (local_row.astype(jnp.int32), (source_group * BLK + offset).astype(jnp.int32))


def draw_tile_rows(key, part):
    return tile_pattern(key)[0]


def draw_tile_cols(key, part):
    return tile_pattern(key)[1]


def draw_tile_count(key, part):
    key = jax.random.fold_in(key, 7)
    row_ids = jnp.arange(N_ROW, dtype=jnp.int32)[:, None]
    col_ids = jnp.arange(N_COL, dtype=jnp.int32)[None, :]
    base_count = TILES_DEV * (row_ids + 1) // N_ROW
    spread = max(1, TILES_DEV // 4)
    jitter = jax.random.randint(key, (N_ROW, N_COL), -spread, spread + 1)
    counts = jnp.clip(base_count + jitter, 1, TILES_DEV)
    fullest = (row_ids == N_ROW - 1) & (col_ids == 0)
    return jnp.where(fullest, TILES_DEV, counts).astype(jnp.int32)


def steps_of(stream_key, dims, cuts, smallest, top_value):
    gain = 1.0
    for position, parts in cuts:
        steps = jax.random.uniform(jax.random.fold_in(jax.random.fold_in(stream_key, 6), position), (parts,), jnp.float32, smallest / len(cuts), top_value / len(cuts))
        gain = gain * jnp.repeat(jnp.exp(steps), dims[position] // parts).reshape((-1,) + (1,) * (len(dims) - 1 - position))
    return gain


def normal_values(own_key, extent, scale, bound, pieces=(), kind=jnp.bfloat16):
    factor_of = steps_of(own_key, extent, pieces, -0.22, 0.18) if pieces else 1.0
    result = jax.random.normal(own_key, extent, jnp.float32) * scale * factor_of
    return jnp.minimum(jnp.maximum(result, -bound), bound).astype(kind)


def setup_inputs(seed: int = 0) -> dict:
    key_list = jax.random.split(jax.random.key(seed), 8)
    return {
        "x_block": normal_values(key_list[0], (VECS, NV), 1.0, 6.0, ((1, 512),), jnp.float32),
        "p_block": normal_values(key_list[1], (VECS, NV), 1.0, 6.0, ((1, 512),), jnp.float32),
        "hp_block": normal_values(key_list[2], (VECS, NV), 1.0, 6.0, ((1, 512),), jnp.float32),
        "tile_rows": draw_tile_rows(jax.random.fold_in(key_list[7], 71), 0),
        "tile_cols": draw_tile_cols(jax.random.fold_in(key_list[7], 71), 0),
        "tile_count": draw_tile_count(jax.random.fold_in(key_list[7], 71), 0),
        "tile_values": normal_values(key_list[6], (N_ROW, N_COL, TILES_DEV, TILE, TILE), (TILE * TILES_DEV // 2) ** -0.5, 0.109375, ((0, 32), (1, 16))),
    }


def apply_hamiltonian(vector_in, tile_rows, tile_cols, tile_count, tile_values):
    rounded = lax.optimization_barrier(vector_in.astype(jnp.bfloat16))
    segments = rounded.astype(jnp.float32).reshape(VECS, NV // TILE, TILE)
    grid_rows = jnp.arange(N_ROW, dtype=jnp.int32)[:, None, None]
    grid_cols = jnp.arange(N_COL, dtype=jnp.int32)[None, :, None]
    global_rows = (grid_rows * ROWB + tile_rows).astype(jnp.int32)
    global_cols = (((tile_cols // BLK) * N_COL + grid_cols) * BLK + tile_cols % BLK).astype(jnp.int32)
    slot_ids = jnp.arange(TILES_DEV, dtype=jnp.int32)[None, None, :]
    live_mask = (slot_ids < tile_count[:, :, None]).astype(jnp.float32)

    def add_row(grid_row, totals):
        row_ids = global_rows[grid_row]
        col_ids = global_cols[grid_row]
        blocks = tile_values[grid_row].astype(jnp.float32)
        weights = live_mask[grid_row][None, :, :, None]
        source_cols = segments[:, col_ids]
        source_rows = segments[:, row_ids]
        forward = jnp.einsum('vctb,ctab->vcta', source_cols, blocks) * weights
        backward = jnp.einsum('vcta,ctab->vctb', source_rows, blocks) * weights
        totals = totals.at[:, row_ids].add(forward)
        return totals.at[:, col_ids].add(backward)

    start_total = jnp.zeros((VECS, NV // TILE, TILE), jnp.float32)
    totals = lax.fori_loop(0, N_ROW, add_row, start_total)
    return totals.reshape(VECS, NV)


def reference(x_block, p_block, hp_block, tile_rows, tile_cols, tile_count, tile_values):
    hx_block = apply_hamiltonian(x_block, tile_rows, tile_cols, tile_count, tile_values)
    theta = jnp.sum(x_block * hx_block, axis=1) / jnp.sum(x_block * x_block, axis=1)
    residual = hx_block - theta[:, None] * x_block
    image = apply_hamiltonian(residual, tile_rows, tile_cols, tile_count, tile_values)
    stacked = jnp.concatenate([x_block, residual, p_block], axis=0)
    images = jnp.concatenate([hx_block, image, hp_block], axis=0)
    gram_s = jnp.dot(stacked, stacked.T, precision=lax.Precision.HIGHEST, preferred_element_type=jnp.float32) / NV
    gram_h = jnp.dot(stacked, images.T, precision=lax.Precision.HIGHEST, preferred_element_type=jnp.float32) / NV
    return residual, image, gram_s, gram_h
```

```python
import jax
import jax.numpy as jnp
from jax import lax
from jax.experimental import pallas as pl
from jax.experimental.pallas import tpu as pltpu
from jax.sharding import PartitionSpec as P

MESH = pl.DeviceIdType.MESH
F32 = jnp.float32
BF16 = jnp.bfloat16
SLOTS = 48
UNROLL = 16
NT = (((1,), (1,)), ((), ()))
PLANE = sorted(
    [(dy, dx) for dy in range(4) for dx in range(4) if (dy, dx) != (0, 0)],
    key=lambda o: -(min(o[0], 4 - o[0]) + min(o[1], 4 - o[1])),
)
RING = [8] + [d for k in range(7, 0, -1) for d in (k, 16 - k)]


def kernel(
    x_hbm, p_hbm, hp_hbm, rows_hbm, cols_hbm, count_hbm, tiles_hbm,
    res_out, img_out, gs_out, gh_out,
    xv, pv, hpv, rows_v, cols_v, rows_s, cols_s, count_s, tiles,
    hot_f, hot_b, prod, rowx, colx, row_send, row_recv, col_send, col_recv,
    part_send, part_recv, stack, images, partner_x,
    th1, th2, early_send, early1, early2, early3, late1, late2,
    local_sem, send_sem, recv_sem,
):
    r = lax.axis_index("row")
    c = lax.axis_index("col")
    zh = lax.rem(r, 2)
    q = lax.div(r, 2)
    y, xx = lax.div(q, 4), lax.rem(q, 4)
    core = lax.rem(c, 2)
    z = zh * 8 + lax.div(c, 2)
    mate = r + 1 - 2 * zh
    partner = (mate, c)
    zslot = zh * 16 + c

    plane_peers = []
    for dy, dx in PLANE:
        other = lax.rem(y + dy, 4) * 4 + lax.rem(xx + dx, 4)
        plane_peers.append((other, (other * 2 + zh, c)))
    line_peers = []
    for k in range(15):
        down = 15 - k
        down = down - jnp.where(down <= c, 1, 0)
        up = k + jnp.where(k >= c, 1, 0)
        other = jnp.where(c < 8, down, up)
        line_peers.append((other, (r, other)))
    ring_peers = []
    for d in RING:
        oz = lax.rem(z + d, 16)
        orow = q * 2 + lax.div(oz, 8)
        for k in range(2):
            ring_peers.append((orow, lax.rem(oz, 8) * 2 + k))
    ring_peers.append((r, c + 1 - 2 * core))

    barrier = pltpu.get_barrier_semaphore()
    for device in ring_peers:
        pl.semaphore_signal(barrier, inc=1, device_id=device, device_id_type=MESH)
    for _, device in plane_peers:
        pl.semaphore_signal(barrier, inc=1, device_id=device, device_id_type=MESH)

    loads = [
        pltpu.make_async_copy(src, dst, local_sem.at[i])
        for i, (src, dst) in enumerate(
            [
                (x_hbm, xv), (rows_hbm, rows_v), (cols_hbm, cols_v), (count_hbm, count_s),
                (rows_hbm, rows_s), (cols_hbm, cols_s), (tiles_hbm, tiles), (p_hbm, pv), (hp_hbm, hpv),
            ]
        )
    ]
    for load in loads:
        load.start()

    def send(src, dst, which, device):
        pltpu.make_async_remote_copy(
            src_ref=src, dst_ref=dst, send_sem=send_sem.at[which], recv_sem=recv_sem.at[which],
            device_id=device, device_id_type=MESH,
        ).start()

    def wait_on(sem, ref):
        pltpu.make_async_copy(ref, ref, sem).wait()

    sent = []

    def arrived(which, ref):
        wait_on(recv_sem.at[which], ref)
        sent.append((which, ref))

    def fold(wide):
        return jnp.concatenate([wide[:, :128], wide[:, 128:]], axis=0)

    def unfold(tall):
        return jnp.concatenate([tall[:8], tall[8:]], axis=1)

    loads[0].wait()
    x_tall = fold(xv[...])
    x_round = x_tall.astype(BF16)
    rowx[0, c] = x_round
    colx[0, r] = x_round

    for i in (1, 2, 3):
        loads[i].wait()
    sub = lax.broadcasted_iota(jnp.int32, (16, SLOTS), 0)
    lane = lax.broadcasted_iota(jnp.int32, (16, SLOTS), 1)
    alive = jnp.where(lane < count_s[0, 0], 1.0, 0.0)
    table = jnp.where(
        sub == 0, rows_v[0].astype(F32), jnp.where(sub == 1, cols_v[0].astype(F32), alive)
    ).astype(BF16)
    spread = jnp.where(
        lax.div(lax.broadcasted_iota(jnp.int32, (SLOTS, SLOTS * 16), 1), 16)
        == lax.broadcasted_iota(jnp.int32, (SLOTS, SLOTS * 16), 0),
        1.0, 0.0,
    ).astype(BF16)
    wide = jnp.dot(table, spread, preferred_element_type=F32).astype(jnp.int32)
    row_id, col_id, on = wide[0:1], wide[1:2], wide[2:3]
    pos = lax.broadcasted_iota(jnp.int32, (1, SLOTS * 16), 1)
    vec = lax.rem(pos, 8)
    half = lax.rem(lax.div(pos, 8), 2)
    key_f = jnp.where((on == 1) & (lax.rem(col_id, 2) == half), row_id * 8 + vec, -1)
    key_b = jnp.where((on == 1) & (lax.rem(row_id, 2) == half), col_id * 8 + vec, -1)
    strip = lax.broadcasted_iota(jnp.int32, (16, SLOTS * 16), 0)

    def fill_f(i, carry):
        hot_f[pl.ds(pl.multiple_of(i * 16, 16), 16), :] = jnp.where(strip + i * 16 == key_f, 1.0, 0.0).astype(BF16)
        return carry

    def fill_b(i, carry):
        hot_b[pl.ds(pl.multiple_of(i * 16, 16), 16), :] = jnp.where(strip + i * 16 == key_b, 1.0, 0.0).astype(BF16)
        return carry

    lax.fori_loop(0, 16, fill_f, 0)
    lax.fori_loop(0, 32, fill_b, 0)
    for i in range(4, 9):
        loads[i].wait()

    pl.semaphore_wait(barrier, len(ring_peers) + len(plane_peers))

    def send_gather(k):
        base = 8 * k
        send(colx.at[k, r], colx.at[k, r], base + 1, partner)
        for _, device in line_peers:
            send(rowx.at[k, c], rowx.at[k, c], base, device)
        for _, device in plane_peers:
            send(colx.at[k, r], colx.at[k, r], base + 2, device)

    def forward_partner(k):
        base = 8 * k
        arrived(base + 1, colx.at[k, mate])
        for _, device in plane_peers:
            send(colx.at[k, mate], colx.at[k, mate], base + 3, device)

    def products(k, index, source, dims):
        def step(i, carry):
            for u in range(UNROLL):
                t = i * UNROLL + u
                block = source[k, lax.div(index[0, 0, t], 2)]
                out = lax.dot_general(block, tiles[0, 0, t], dims, preferred_element_type=F32)
                prod[pl.ds(pl.multiple_of(t * 16, 16), 16), :] = out.astype(BF16)
            return carry

        lax.fori_loop(0, SLOTS // UNROLL, step, 0)

    def transposed_part(k):
        base = 8 * k
        arrived(base, rowx.at[k, pl.ds(0, 15)])
        products(k, rows_s, rowx, (((1,), (0,)), ((), ())))
        for g in range(4):
            part = jnp.dot(hot_b[pl.ds(g * 128, 128), :], prod[...], preferred_element_type=F32)
            col_send[k, pl.ds(g * 4, 4)] = part.astype(BF16).reshape(4, 32, 128)
        col_recv[k, q] = col_send[k, q]
        for other, device in plane_peers:
            send(col_send.at[k, other], col_recv.at[k, q], base + 4, device)

    def forward_part(k):
        base = 8 * k
        arrived(base + 2, colx.at[k, pl.ds(0, 15)])
        arrived(base + 3, colx.at[k, pl.ds(0, 15)])
        products(k, cols_s, colx, NT)
        for g in range(2):
            part = jnp.dot(hot_f[pl.ds(g * 128, 128), :], prod[...], preferred_element_type=F32)
            row_send[k, pl.ds(g * 8, 8)] = part.astype(BF16).reshape(8, 16, 128)
        row_recv[k, c] = row_send[k, c]
        for other, device in line_peers:
            send(row_send.at[k, other], row_recv.at[k, c], base + 5, device)

    def total(ref, k, n):
        out = ref[k, 0].astype(F32)
        for i in range(1, n):
            out = out + ref[k, i].astype(F32)
        return out

    def column_sums(k):
        base = 8 * k
        arrived(base + 4, col_recv.at[k, pl.ds(0, 15)])
        both = total(col_recv, k, 16)
        mine = jnp.where(zh == 0, both[:16], both[16:])
        theirs = jnp.where(zh == 0, both[16:], both[:16])
        part_send[k] = theirs
        send(part_send.at[k], part_recv.at[k], base + 6, partner)
        return mine, theirs

    def finish(k, mine):
        base = 8 * k
        arrived(base + 5, row_recv.at[k, pl.ds(0, 15)])
        out = mine + total(row_recv, k, 16)
        arrived(base + 6, part_recv.at[k])
        return out + part_recv[k]

    send_gather(0)
    send(xv, partner_x, 16, partner)
    stack[0:8] = xv[...]
    stack[16:24] = pv[...]
    images[24:32] = hpv[...]
    forward_partner(0)
    transposed_part(0)
    forward_part(0)
    mine, theirs = column_sums(0)

    arrived(16, partner_x)
    weighted = x_tall * mine + fold(partner_x[...]) * theirs
    squared = x_tall * x_tall
    num = jnp.sum(weighted[:8] + weighted[8:], axis=1, keepdims=True)
    den = jnp.sum(squared[:8] + squared[8:], axis=1, keepdims=True)
    sub8 = lax.broadcasted_iota(jnp.int32, (8, 128), 0)
    lane8 = lax.broadcasted_iota(jnp.int32, (8, 128), 1)
    placed = jnp.where(lane8 == sub8, num, jnp.where(lane8 == sub8 + 8, den, 0.0))
    th1[q] = jnp.sum(placed, axis=0, keepdims=True)
    for _, device in plane_peers:
        send(th1.at[q], th1.at[q], 17, device)
    arrived(17, th1.at[pl.ds(0, 15)])
    acc = th1[0]
    for i in range(1, 16):
        acc = acc + th1[i]
    th2[zslot] = acc
    for device in ring_peers:
        send(th2.at[zslot], th2.at[zslot], 18, device)
    hx_tall = finish(0, mine)
    arrived(18, th2.at[pl.ds(0, 31)])
    acc = th2[0]
    for i in range(1, 32):
        acc = acc + th2[i]
    num = 2.0 * jnp.sum(jnp.where(lane8 == sub8, acc, 0.0), axis=1, keepdims=True)
    den = jnp.sum(jnp.where(lane8 == sub8 + 8, acc, 0.0), axis=1, keepdims=True)
    theta = num / den
    theta_tall = jnp.concatenate([theta, theta], axis=0)
    res_tall = hx_tall - theta_tall * x_tall
    res_round = res_tall.astype(BF16)
    rowx[1, c] = res_round
    colx[1, r] = res_round

    send_gather(1)
    residual = unfold(res_tall)
    res_out[...] = residual
    stack[8:16] = residual
    images[0:24] = stack[...]
    images[32:40] = unfold(hx_tall)
    early = lax.dot_general(
        stack[...], images[...], NT, precision=lax.Precision.HIGHEST, preferred_element_type=F32
    )
    early = jnp.concatenate([early, jnp.zeros((24, 88), F32)], axis=1)
    for i in range(12):
        early_send[i] = early[2 * i : 2 * i + 2]
    for i in range(12, 16):
        early_send[i] = jnp.zeros((2, 128), F32)
    early1[q] = early_send[q]
    for other, device in plane_peers:
        send(early_send.at[other], early1.at[q], 19, device)
    forward_partner(1)
    transposed_part(1)
    arrived(19, early1.at[pl.ds(0, 15)])
    acc = early1[0]
    for i in range(1, 16):
        acc = acc + early1[i]
    early2[zslot] = acc
    for device in ring_peers:
        send(early2.at[zslot], early2.at[zslot], 20, device)
    forward_part(1)
    mine, theirs = column_sums(1)
    arrived(20, early2.at[pl.ds(0, 31)])
    acc = early2[0]
    for i in range(1, 32):
        acc = acc + early2[i]
    early3[q] = acc
    for _, device in plane_peers:
        send(early3.at[q], early3.at[q], 21, device)
    img_tall = finish(1, mine)
    image = unfold(img_tall)
    img_out[...] = image

    late = lax.dot_general(
        stack[...], image, NT, precision=lax.Precision.HIGHEST, preferred_element_type=F32
    )
    late = jnp.concatenate([late, jnp.zeros((24, 120), F32)], axis=1)
    packed = late[0:8] + pltpu.roll(late[8:16], 8, 1) + pltpu.roll(late[16:24], 16, 1)
    lines = jnp.where(lax.rem(sub8, 4) == 0, packed, 0.0)
    for k in range(1, 4):
        lines = lines + jnp.where(lax.rem(sub8, 4) == k, pltpu.roll(packed, 32 * k, 1), 0.0)
    late1[q] = jnp.concatenate(
        [jnp.sum(lines[0:4], axis=0, keepdims=True), jnp.sum(lines[4:8], axis=0, keepdims=True)], axis=0
    )
    for _, device in plane_peers:
        send(late1.at[q], late1.at[q], 22, device)
    arrived(22, late1.at[pl.ds(0, 15)])
    acc = late1[0]
    for i in range(1, 16):
        acc = acc + late1[i]
    late2[zslot] = acc
    for device in ring_peers:
        send(late2.at[zslot], late2.at[zslot], 23, device)

    cells = 1.0 / 131072.0
    arrived(21, early3.at[pl.ds(0, 15)])
    rows = [early3[i] for i in range(12)]
    early = jnp.concatenate(rows, axis=0) * cells
    gs_out[...] = early[:, :24]
    shifted = pltpu.roll(early, 128 - 32, 1)
    hp_part = pltpu.roll(early, 128 - 8, 1)

    arrived(23, late2.at[pl.ds(0, 31)])
    acc = late2[0]
    for i in range(1, 32):
        acc = acc + late2[i]
    acc = acc * cells
    spread8 = jnp.where(sub8 < 4, acc[0:1], acc[1:2])
    packed = jnp.where(lax.rem(sub8, 4) == 0, spread8, 0.0)
    for k in range(1, 4):
        packed = packed + jnp.where(lax.rem(sub8, 4) == k, pltpu.roll(spread8, 128 - 32 * k, 1), 0.0)
    for a in range(3):
        block = pltpu.roll(packed, 136 - 8 * a if a > 1 else 8 - 8 * a, 1) if a != 1 else packed
        low = shifted[8 * a : 8 * a + 8]
        high = hp_part[8 * a : 8 * a + 8]
        block = jnp.where(lane8 < 8, low, jnp.where(lane8 < 16, block, high))
        gh_out[8 * a : 8 * a + 8, :] = block[:, :24]

    for which, ref in sent:
        wait_on(send_sem.at[which], ref)


def solution(mesh):
    def body(x_block, p_block, hp_block, tile_rows, tile_cols, tile_count, tile_values):
        any_spec = pl.BlockSpec(memory_space=pl.ANY)
        vmem = pl.BlockSpec(memory_space=pltpu.VMEM)
        return pl.pallas_call(
            kernel,
            out_shape=(
                jax.ShapeDtypeStruct((8, 256), F32),
                jax.ShapeDtypeStruct((8, 256), F32),
                jax.ShapeDtypeStruct((24, 24), F32),
                jax.ShapeDtypeStruct((24, 24), F32),
            ),
            in_specs=[any_spec] * 7,
            out_specs=(vmem,) * 4,
            scratch_shapes=[
                pltpu.VMEM((8, 256), F32), pltpu.VMEM((8, 256), F32), pltpu.VMEM((8, 256), F32),
                pltpu.VMEM((1, 1, SLOTS), jnp.int32), pltpu.VMEM((1, 1, SLOTS), jnp.int32),
                pltpu.SMEM((1, 1, SLOTS), jnp.int32), pltpu.SMEM((1, 1, SLOTS), jnp.int32),
                pltpu.SMEM((1, 1), jnp.int32),
                pltpu.VMEM((1, 1, SLOTS, 128, 128), BF16),
                pltpu.VMEM((256, SLOTS * 16), BF16), pltpu.VMEM((512, SLOTS * 16), BF16),
                pltpu.VMEM((SLOTS * 16, 128), BF16),
                pltpu.VMEM((2, 16, 16, 128), BF16), pltpu.VMEM((2, 32, 16, 128), BF16),
                pltpu.VMEM((2, 16, 16, 128), BF16), pltpu.VMEM((2, 16, 16, 128), BF16),
                pltpu.VMEM((2, 16, 32, 128), BF16), pltpu.VMEM((2, 16, 32, 128), BF16),
                pltpu.VMEM((2, 16, 128), F32), pltpu.VMEM((2, 16, 128), F32),
                pltpu.VMEM((24, 256), F32), pltpu.VMEM((40, 256), F32), pltpu.VMEM((8, 256), F32),
                pltpu.VMEM((16, 1, 128), F32), pltpu.VMEM((32, 1, 128), F32),
                pltpu.VMEM((16, 2, 128), F32), pltpu.VMEM((16, 2, 128), F32),
                pltpu.VMEM((32, 2, 128), F32), pltpu.VMEM((16, 2, 128), F32),
                pltpu.VMEM((16, 2, 128), F32), pltpu.VMEM((32, 2, 128), F32),
                pltpu.SemaphoreType.DMA((9,)), pltpu.SemaphoreType.DMA((24,)), pltpu.SemaphoreType.DMA((24,)),
            ],
            compiler_params=pltpu.CompilerParams(
                collective_id=0, has_side_effects=True, vmem_limit_bytes=32 * 1024 * 1024
            ),
        )(x_block, p_block, hp_block, tile_rows, tile_cols, tile_count, tile_values)

    in_specs = (
        P(None, ("row", "col")),
        P(None, ("row", "col")),
        P(None, ("row", "col")),
        P("row", "col", None),
        P("row", "col", None),
        P("row", "col"),
        P("row", "col", None, None, None),
    )
    out_specs = (P(None, ("row", "col")), P(None, ("row", "col")), P(), P())
    return jax.shard_map(body, mesh=mesh, in_specs=in_specs, out_specs=out_specs, check_vma=False)
```

```python
import jax
import jax.numpy as jnp
from jax import lax
from jax.experimental import pallas as pl
from jax.experimental.pallas import tpu as pltpu
from jax.sharding import PartitionSpec as P

MESH = pl.DeviceIdType.MESH
F32 = jnp.float32
BF16 = jnp.bfloat16
SLOTS = 48
UNROLL = 16
VMEM_LIMIT = 60 * 1024 * 1024
NN = (((1,), (0,)), ((), ()))
NT = (((1,), (1,)), ((), ()))
def kernel(
    x_hbm, p_hbm, hp_hbm, rows_hbm, cols_hbm, count_hbm, tiles_hbm,
    res_out, img_out, gs_out, gh_out,
    xv, pv, hpv, rows_v, cols_v, rows_s, cols_s, count_s, tiles,
    hot_f, hot_b, prod, rowx, colx, row_send, row_recv, col_send, col_recv,
    part_send, part_recv, stack, images, partner_x, partner_p, rowp, colp_send, colp_recv,
    th1, th2, early_send, early1, early2, early3, late1, late2,
    local_sem, send_sem, recv_sem,
):
    r = lax.axis_index("row")
    c = lax.axis_index("col")
    zh = lax.rem(r, 2)
    q = lax.div(r, 2)
    y, xx = lax.div(q, 4), lax.rem(q, 4)
    core = lax.rem(c, 2)
    z = zh * 8 + lax.div(c, 2)
    mate = r + 1 - 2 * zh
    partner = (mate, c)
    zslot = zh * 16 + c

    def each_plane(act):
        def step(i, carry):
            a, b = lax.div(i, 4), lax.rem(i, 4)
            dy = jnp.where(a < 2, 2 - a, 9 - 3 * a)
            dx = jnp.where(b < 2, 2 - b, 9 - 3 * b)
            other = lax.rem(y + dy, 4) * 4 + lax.rem(xx + dx, 4)
            act(other, (other * 2 + zh, c))
            return carry

        lax.fori_loop(0, 15, step, 0)

    def each_line(act):
        def step(i, carry):
            down = 15 - i - jnp.where(15 - i <= c, 1, 0)
            up = i + jnp.where(i >= c, 1, 0)
            other = jnp.where(c < 8, down, up)
            act(other, (r, other))
            return carry

        lax.fori_loop(0, 15, step, 0)

    def each_ring(act):
        def step(i, carry):
            m = lax.div(i, 2)
            s = lax.div(m + 1, 2)
            d = 8 + jnp.where(lax.rem(m, 2) == 0, s, -s)
            oz = lax.rem(z + d, 16)
            k = jnp.where(m == 15, 1 - core, lax.rem(i, 2))
            act((q * 2 + lax.div(oz, 8), lax.rem(oz, 8) * 2 + k))
            return carry

        lax.fori_loop(0, 31, step, 0)

    barrier = pltpu.get_barrier_semaphore()

    def greet(device):
        pl.semaphore_signal(barrier, inc=1, device_id=device, device_id_type=MESH)

    each_ring(greet)
    each_plane(lambda other, device: greet(device))

    loads = [
        pltpu.make_async_copy(src, dst, local_sem.at[i])
        for i, (src, dst) in enumerate(
            [
                (x_hbm, xv), (rows_hbm, rows_v), (cols_hbm, cols_v), (count_hbm, count_s),
                (rows_hbm, rows_s), (cols_hbm, cols_s), (tiles_hbm, tiles), (p_hbm, pv), (hp_hbm, hpv),
            ]
        )
    ]
    for load in loads:
        load.start()

    def send(src, dst, which, device):
        pltpu.make_async_remote_copy(
            src_ref=src, dst_ref=dst, send_sem=send_sem.at[which], recv_sem=recv_sem.at[which],
            device_id=device, device_id_type=MESH,
        ).start()

    def wait_on(sem, ref):
        pltpu.make_async_copy(ref, ref, sem).wait()

    sent = []

    def arrived(which, ref):
        wait_on(recv_sem.at[which], ref)
        sent.append((which, ref))

    def exact(a, b):
        return lax.dot_general(a, b, NT, precision=lax.Precision.HIGHEST, preferred_element_type=F32)

    def fold(wide):
        return jnp.concatenate([wide[:, :128], wide[:, 128:]], axis=0)

    def unfold(tall):
        return jnp.concatenate([tall[:8], tall[8:]], axis=1)

    loads[0].wait()
    x_tall = fold(xv[...])
    x_round = x_tall.astype(BF16)
    rowx[0, c] = x_round
    loads[7].wait()
    rowp[c] = fold(pv[...]).astype(BF16)
    colx[0, r] = x_round

    for i in (1, 2, 3):
        loads[i].wait()
    sub = lax.broadcasted_iota(jnp.int32, (16, SLOTS), 0)
    lane = lax.broadcasted_iota(jnp.int32, (16, SLOTS), 1)
    alive = jnp.where(lane < count_s[0, 0], 1.0, 0.0)
    table = jnp.where(
        sub == 0, rows_v[0].astype(F32), jnp.where(sub == 1, cols_v[0].astype(F32), alive)
    ).astype(BF16)
    spread = jnp.where(
        lax.div(lax.broadcasted_iota(jnp.int32, (SLOTS, SLOTS * 16), 1), 16)
        == lax.broadcasted_iota(jnp.int32, (SLOTS, SLOTS * 16), 0),
        1.0, 0.0,
    ).astype(BF16)
    wide = jnp.dot(table, spread, preferred_element_type=F32).astype(jnp.int32)
    row_id, col_id, on = wide[0:1], wide[1:2], wide[2:3]
    pos = lax.broadcasted_iota(jnp.int32, (1, SLOTS * 16), 1)
    vec = lax.rem(pos, 8)
    half = lax.rem(lax.div(pos, 8), 2)
    key_f = jnp.where((on == 1) & (lax.rem(col_id, 2) == half), row_id * 8 + vec, -1)
    key_b = jnp.where((on == 1) & (lax.rem(row_id, 2) == half), col_id * 8 + vec, -1)
    strip = lax.broadcasted_iota(jnp.int32, (16, SLOTS * 16), 0)

    def fill_f(i, carry):
        hot_f[pl.ds(pl.multiple_of(i * 16, 16), 16), :] = jnp.where(strip + i * 16 == key_f, 1.0, 0.0).astype(BF16)
        return carry

    def fill_b(i, carry):
        hot_b[pl.ds(pl.multiple_of(i * 16, 16), 16), :] = jnp.where(strip + i * 16 == key_b, 1.0, 0.0).astype(BF16)
        return carry

    lax.fori_loop(0, 16, fill_f, 0)
    lax.fori_loop(0, 32, fill_b, 0)
    for i in (4, 5, 6, 8):
        loads[i].wait()

    pl.semaphore_wait(barrier, 46)

    def send_gather(k):
        base = 8 * k
        send(colx.at[k, r], colx.at[k, r], base + 1, partner)
        each_line(lambda other, device: send(rowx.at[k, c], rowx.at[k, c], base, device))
        each_plane(lambda other, device: send(colx.at[k, r], colx.at[k, r], base + 2, device))

    def forward_partner(k):
        base = 8 * k
        arrived(base + 1, colx.at[k, mate])
        each_plane(lambda other, device: send(colx.at[k, mate], colx.at[k, mate], base + 3, device))

    def products(index, source, dims):
        def step(i, carry):
            for u in range(UNROLL):
                t = i * UNROLL + u
                block = source[lax.div(index[0, 0, t], 2)]
                out = lax.dot_general(block, tiles[0, 0, t], dims, preferred_element_type=F32)
                prod[pl.ds(pl.multiple_of(t * 16, 16), 16), :] = out.astype(BF16)
            return carry

        lax.fori_loop(0, SLOTS // UNROLL, step, 0)

    def to_columns(out):
        for g in range(4):
            part = jnp.dot(hot_b[pl.ds(g * 128, 128), :], prod[...], preferred_element_type=F32)
            out[pl.ds(g * 4, 4)] = part.astype(BF16).reshape(4, 32, 128)

    def transposed_part(k):
        base = 8 * k
        arrived(base, rowx.at[k, pl.ds(0, 15)])
        products(rows_s, rowx.at[k], NN)
        to_columns(col_send.at[k])
        col_recv[k, q] = col_send[k, q]
        each_plane(lambda other, device: send(col_send.at[k, other], col_recv.at[k, q], base + 4, device))

    def forward_part(k):
        base = 8 * k
        arrived(base + 2, colx.at[k, pl.ds(0, 15)])
        arrived(base + 3, colx.at[k, pl.ds(0, 15)])
        products(cols_s, colx.at[k], NT)
        for g in range(2):
            part = jnp.dot(hot_f[pl.ds(g * 128, 128), :], prod[...], preferred_element_type=F32)
            row_send[k, pl.ds(g * 8, 8)] = part.astype(BF16).reshape(8, 16, 128)
        row_recv[k, c] = row_send[k, c]
        each_line(lambda other, device: send(row_send.at[k, other], row_recv.at[k, c], base + 5, device))

    def total(ref, n):
        out = ref[0].astype(F32)
        for i in range(1, n):
            out = out + ref[i].astype(F32)
        return out

    def split(both):
        return jnp.where(zh == 0, both[:16], both[16:]), jnp.where(zh == 0, both[16:], both[:16])

    def column_sums(k):
        base = 8 * k
        arrived(base + 4, col_recv.at[k, pl.ds(0, 15)])
        mine, theirs = split(total(col_recv.at[k], 16))
        part_send[k] = theirs
        send(part_send.at[k], part_recv.at[k], base + 6, partner)
        return mine, theirs

    def finish(k, mine):
        base = 8 * k
        arrived(base + 5, row_recv.at[k, pl.ds(0, 15)])
        out = mine + total(row_recv.at[k], 16)
        arrived(base + 6, part_recv.at[k])
        return out + part_recv[k]

    send_gather(0)
    send(xv, partner_x, 16, partner)
    send(pv, partner_p, 24, partner)
    each_line(lambda other, device: send(rowp.at[c], rowp.at[c], 25, device))
    stack[0:8] = xv[...]
    stack[16:24] = pv[...]
    images[24:32] = hpv[...]
    forward_partner(0)
    transposed_part(0)
    forward_part(0)
    mine, theirs = column_sums(0)

    arrived(16, partner_x)
    weighted = x_tall * mine + fold(partner_x[...]) * theirs
    squared = x_tall * x_tall
    num = jnp.sum(weighted[:8] + weighted[8:], axis=1, keepdims=True)
    den = jnp.sum(squared[:8] + squared[8:], axis=1, keepdims=True)
    sub8 = lax.broadcasted_iota(jnp.int32, (8, 128), 0)
    lane8 = lax.broadcasted_iota(jnp.int32, (8, 128), 1)
    placed = jnp.where(lane8 == sub8, num, jnp.where(lane8 == sub8 + 8, den, 0.0))
    th1[q] = jnp.sum(placed, axis=0, keepdims=True)
    each_plane(lambda other, device: send(th1.at[q], th1.at[q], 17, device))
    arrived(17, th1.at[pl.ds(0, 15)])
    acc = total(th1, 16)
    th2[zslot] = acc
    each_ring(lambda device: send(th2.at[zslot], th2.at[zslot], 18, device))

    arrived(25, rowp.at[pl.ds(0, 15)])
    products(rows_s, rowp, NN)
    to_columns(colp_send)
    colp_recv[q] = colp_send[q]
    each_plane(lambda other, device: send(colp_send.at[other], colp_recv.at[q], 26, device))

    hx_tall = finish(0, mine)
    arrived(18, th2.at[pl.ds(0, 31)])
    acc = total(th2, 32)
    num = 2.0 * jnp.sum(jnp.where(lane8 == sub8, acc, 0.0), axis=1, keepdims=True)
    den = jnp.sum(jnp.where(lane8 == sub8 + 8, acc, 0.0), axis=1, keepdims=True)
    theta = num / den
    theta_tall = jnp.concatenate([theta, theta], axis=0)
    res_tall = hx_tall - theta_tall * x_tall
    res_round = res_tall.astype(BF16)
    rowx[1, c] = res_round
    colx[1, r] = res_round

    send_gather(1)
    residual = unfold(res_tall)
    res_out[...] = residual
    stack[8:16] = residual
    stack[24:32] = unfold(hx_tall)
    images[0:24] = stack[0:24]
    images[32:40] = stack[24:32]
    images[40:48] = unfold(res_round.astype(F32))
    early = exact(stack[...], images[...])
    early = jnp.concatenate([early, jnp.zeros((32, 80), F32)], axis=1)
    for i in range(16):
        early_send[i] = early[2 * i : 2 * i + 2]
    early1[q] = early_send[q]
    each_plane(lambda other, device: send(early_send.at[other], early1.at[q], 19, device))
    forward_partner(1)
    transposed_part(1)
    arrived(19, early1.at[pl.ds(0, 15)])
    acc = total(early1, 16)
    early2[zslot] = acc
    each_ring(lambda device: send(early2.at[zslot], early2.at[zslot], 20, device))
    forward_part(1)
    mine, theirs = column_sums(1)

    arrived(26, colp_recv.at[pl.ds(0, 15)])
    arrived(24, partner_p)
    pair = jnp.concatenate([unfold(mine), unfold(theirs)], axis=1)
    res_pair = jnp.concatenate([unfold(res_round.astype(F32)), unfold(colx[1, mate].astype(F32))], axis=1)
    p_pair = jnp.concatenate([pv[...], partner_p[...]], axis=1)
    hp_mine, hp_theirs = split(total(colp_recv, 16))
    hp_pair = jnp.concatenate([unfold(hp_mine), unfold(hp_theirs)], axis=1)
    late = exact(jnp.concatenate([res_pair, p_pair], axis=0), pair)
    late = late + exact(jnp.concatenate([pair, hp_pair], axis=0), res_pair)
    late = jnp.concatenate([late, jnp.zeros((16, 120), F32)], axis=1)
    late1[q] = jnp.sum(pltpu.roll(late, 0, 1, stride=8, stride_axis=0), axis=0, keepdims=True)
    each_plane(lambda other, device: send(late1.at[q], late1.at[q], 22, device))

    arrived(20, early2.at[pl.ds(0, 31)])
    early3[q] = total(early2, 32)
    each_plane(lambda other, device: send(early3.at[q], early3.at[q], 21, device))
    arrived(22, late1.at[pl.ds(0, 15)])
    late2[zslot] = total(late1, 16)
    each_ring(lambda device: send(late2.at[zslot], late2.at[zslot], 23, device))

    img_out[...] = unfold(finish(1, mine))
    cells = 1.0 / 131072.0
    place = jnp.where(
        lax.broadcasted_iota(jnp.int32, (128, 128), 0) == 8 + lax.rem(lax.broadcasted_iota(jnp.int32, (128, 128), 1), 8),
        1.0, 0.0,
    )
    arrived(21, early3.at[pl.ds(0, 15)])
    early = jnp.concatenate([early3[i] for i in range(16)], axis=0) * cells
    gs_out[...] = early[:24, :24]
    hx_part = pltpu.roll(early[:24], 128 - 32, 1)
    hp_part = pltpu.roll(early[:24], 128 - 8, 1)
    image_x = pltpu.roll(early[24:32], 128 - 32, 1)

    arrived(23, late2.at[pl.ds(0, 31)])
    late = total(late2, 32) * cells
    lane16 = lax.broadcasted_iota(jnp.int32, (16, 128), 1)
    late = jnp.where(lax.div(lane16, 8) == lax.broadcasted_iota(jnp.int32, (16, 128), 0), late, 0.0)
    late = exact(late, place)
    image_part = jnp.concatenate([image_x, late], axis=0)
    lane24 = lax.broadcasted_iota(jnp.int32, (24, 128), 1)
    whole = jnp.where(lane24 < 8, hx_part, jnp.where(lane24 < 16, image_part, hp_part))
    gh_out[...] = whole[:, :24]

    for which, ref in sent:
        wait_on(send_sem.at[which], ref)


def deliver(a, b, c, d, out_a, out_b, out_c, out_d, sem):
    pairs = ((a, out_a), (b, out_b), (c, out_c), (d, out_d))
    copies = [pltpu.make_async_copy(src, dst, sem.at[i]) for i, (src, dst) in enumerate(pairs)]
    for copy in copies:
        copy.start()
    for copy in copies:
        copy.wait()


def solution(mesh):
    def body(x_block, p_block, hp_block, tile_rows, tile_cols, tile_count, tile_values):
        any_spec = pl.BlockSpec(memory_space=pl.ANY)
        hbm = pl.BlockSpec(memory_space=pltpu.HBM)
        vmem = pl.BlockSpec(memory_space=pltpu.VMEM)
        shapes = (
            jax.ShapeDtypeStruct((8, 256), F32),
            jax.ShapeDtypeStruct((8, 256), F32),
            jax.ShapeDtypeStruct((24, 24), F32),
            jax.ShapeDtypeStruct((24, 24), F32),
        )
        results = pl.pallas_call(
            kernel,
            out_shape=shapes,
            in_specs=[any_spec] * 7,
            out_specs=(vmem,) * 4,
            scratch_shapes=[
                pltpu.VMEM((8, 256), F32), pltpu.VMEM((8, 256), F32), pltpu.VMEM((8, 256), F32),
                pltpu.VMEM((1, 1, SLOTS), jnp.int32), pltpu.VMEM((1, 1, SLOTS), jnp.int32),
                pltpu.SMEM((1, 1, SLOTS), jnp.int32), pltpu.SMEM((1, 1, SLOTS), jnp.int32),
                pltpu.SMEM((1, 1), jnp.int32),
                pltpu.VMEM((1, 1, SLOTS, 128, 128), BF16),
                pltpu.VMEM((256, SLOTS * 16), BF16), pltpu.VMEM((512, SLOTS * 16), BF16),
                pltpu.VMEM((SLOTS * 16, 128), BF16),
                pltpu.VMEM((2, 16, 16, 128), BF16), pltpu.VMEM((2, 32, 16, 128), BF16),
                pltpu.VMEM((2, 16, 16, 128), BF16), pltpu.VMEM((2, 16, 16, 128), BF16),
                pltpu.VMEM((2, 16, 32, 128), BF16), pltpu.VMEM((2, 16, 32, 128), BF16),
                pltpu.VMEM((2, 16, 128), F32), pltpu.VMEM((2, 16, 128), F32),
                pltpu.VMEM((32, 256), F32), pltpu.VMEM((48, 256), F32),
                pltpu.VMEM((8, 256), F32), pltpu.VMEM((8, 256), F32),
                pltpu.VMEM((16, 16, 128), BF16), pltpu.VMEM((16, 32, 128), BF16), pltpu.VMEM((16, 32, 128), BF16),
                pltpu.VMEM((16, 1, 128), F32), pltpu.VMEM((32, 1, 128), F32),
                pltpu.VMEM((16, 2, 128), F32), pltpu.VMEM((16, 2, 128), F32),
                pltpu.VMEM((32, 2, 128), F32), pltpu.VMEM((16, 2, 128), F32),
                pltpu.VMEM((16, 1, 128), F32), pltpu.VMEM((32, 1, 128), F32),
                pltpu.SemaphoreType.DMA((9,)), pltpu.SemaphoreType.DMA((27,)), pltpu.SemaphoreType.DMA((27,)),
            ],
            compiler_params=pltpu.CompilerParams(
                collective_id=0, has_side_effects=True, vmem_limit_bytes=VMEM_LIMIT
            ),
        )(x_block, p_block, hp_block, tile_rows, tile_cols, tile_count, tile_values)
        return pl.pallas_call(
            deliver,
            out_shape=shapes,
            in_specs=[any_spec] * 4,
            out_specs=(any_spec,) * 4,
            scratch_shapes=[pltpu.SemaphoreType.DMA((4,))],
        )(*results)

    in_specs = (
        P(None, ("row", "col")),
        P(None, ("row", "col")),
        P(None, ("row", "col")),
        P("row", "col", None),
        P("row", "col", None),
        P("row", "col"),
        P("row", "col", None, None, None),
    )
    out_specs = (P(None, ("row", "col")), P(None, ("row", "col")), P(), P())
    return jax.shard_map(body, mesh=mesh, in_specs=in_specs, out_specs=out_specs, check_vma=False)
```

```python
import jax
import jax.numpy as jnp
from jax import lax
from jax.experimental import pallas as pl
from jax.experimental.pallas import tpu as pltpu
from jax.sharding import PartitionSpec as P

MESH = pl.DeviceIdType.MESH
F32 = jnp.float32
BF16 = jnp.bfloat16
SLOTS = 48
UNROLL = 48
VMEM_LIMIT = 32 * 1024 * 1024
NN = (((1,), (0,)), ((), ()))
NT = (((1,), (1,)), ((), ()))
def kernel(
    x_hbm, p_hbm, hp_hbm, rows_hbm, cols_hbm, count_hbm, tiles_hbm,
    res_out, img_out, gs_out, gh_out,
    xv, pv, hpv, rows_v, cols_v, rows_s, cols_s, count_s, tiles,
    hot_f, hot_b, prod, rowx0, rowx1, colx0, colx1, row_send, row_recv, col_send, col_recv,
    part_send, part_recv, stack, images, partner_x, partner_p, rowp, colp_send, colp_recv,
    th1, th2, early_send, early1, early2, early3, late1, late2,
    local_sem, send_sem, recv_sem,
):
    rowx, colx = (rowx0, rowx1), (colx0, colx1)
    r = lax.axis_index("row")
    c = lax.axis_index("col")
    zh = lax.rem(r, 2)
    q = lax.div(r, 2)
    y, xx = lax.div(q, 4), lax.rem(q, 4)
    core = lax.rem(c, 2)
    z = zh * 8 + lax.div(c, 2)
    mate = r + 1 - 2 * zh
    partner = (mate, c)
    zslot = zh * 16 + c

    def each_plane(act):
        def step(i, carry):
            a, b = lax.div(i, 4), lax.rem(i, 4)
            dy = jnp.where(a < 2, 2 - a, 9 - 3 * a)
            dx = jnp.where(b < 2, 2 - b, 9 - 3 * b)
            other = lax.rem(y + dy, 4) * 4 + lax.rem(xx + dx, 4)
            act(other, (other * 2 + zh, c))
            return carry

        lax.fori_loop(0, 15, step, 0)

    def each_line(act):
        def step(i, carry):
            down = 15 - i - jnp.where(15 - i <= c, 1, 0)
            up = i + jnp.where(i >= c, 1, 0)
            other = jnp.where(c < 8, down, up)
            act(other, (r, other))
            return carry

        lax.fori_loop(0, 15, step, 0)

    def each_ring(act):
        def step(i, carry):
            m = lax.div(i, 2)
            s = lax.div(m + 1, 2)
            d = 8 + jnp.where(lax.rem(m, 2) == 0, s, -s)
            oz = lax.rem(z + d, 16)
            k = jnp.where(m == 15, 1 - core, lax.rem(i, 2))
            act((q * 2 + lax.div(oz, 8), lax.rem(oz, 8) * 2 + k))
            return carry

        lax.fori_loop(0, 31, step, 0)

    barrier = pltpu.get_barrier_semaphore()

    def greet(device):
        pl.semaphore_signal(barrier, inc=1, device_id=device, device_id_type=MESH)

    each_ring(greet)
    each_plane(lambda other, device: greet(device))

    loads = [
        pltpu.make_async_copy(src, dst, local_sem.at[i])
        for i, (src, dst) in enumerate(
            [
                (x_hbm, xv), (rows_hbm, rows_v), (cols_hbm, cols_v), (count_hbm, count_s),
                (rows_hbm, rows_s), (cols_hbm, cols_s), (tiles_hbm, tiles), (p_hbm, pv), (hp_hbm, hpv),
            ]
        )
    ]
    for load in loads:
        load.start()

    def send(src, dst, which, device):
        pltpu.make_async_remote_copy(
            src_ref=src, dst_ref=dst, send_sem=send_sem.at[which], recv_sem=recv_sem.at[which],
            device_id=device, device_id_type=MESH,
        ).start()

    def wait_on(sem, ref):
        pltpu.make_async_copy(ref, ref, sem).wait()

    sent = []

    def arrived(which, ref):
        wait_on(recv_sem.at[which], ref)
        sent.append((which, ref))

    def exact(a, b):
        return lax.dot_general(a, b, NT, precision=lax.Precision.HIGHEST, preferred_element_type=F32)

    def fold(wide):
        return jnp.concatenate([wide[:, :128], wide[:, 128:]], axis=0)

    def unfold(tall):
        return jnp.concatenate([tall[:8], tall[8:]], axis=1)

    loads[0].wait()
    x_tall = fold(xv[...])
    x_round = x_tall.astype(BF16)
    rowx[0][c] = x_round
    loads[7].wait()
    rowp[c] = fold(pv[...]).astype(BF16)
    colx[0][r] = x_round

    for i in (1, 2, 3):
        loads[i].wait()
    sub = lax.broadcasted_iota(jnp.int32, (16, SLOTS), 0)
    lane = lax.broadcasted_iota(jnp.int32, (16, SLOTS), 1)
    alive = jnp.where(lane < count_s[0, 0], 1.0, 0.0)
    table = jnp.where(
        sub == 0, rows_v[0].astype(F32), jnp.where(sub == 1, cols_v[0].astype(F32), alive)
    ).astype(BF16)
    spread = jnp.where(
        lax.div(lax.broadcasted_iota(jnp.int32, (SLOTS, SLOTS * 16), 1), 16)
        == lax.broadcasted_iota(jnp.int32, (SLOTS, SLOTS * 16), 0),
        1.0, 0.0,
    ).astype(BF16)
    wide = jnp.dot(table, spread, preferred_element_type=F32).astype(jnp.int32)
    row_id, col_id, on = wide[0:1], wide[1:2], wide[2:3]
    pos = lax.broadcasted_iota(jnp.int32, (1, SLOTS * 16), 1)
    vec = lax.rem(pos, 8)
    half = lax.rem(lax.div(pos, 8), 2)
    key_f = jnp.where((on == 1) & (lax.rem(col_id, 2) == half), row_id * 8 + vec, -1)
    key_b = jnp.where((on == 1) & (lax.rem(row_id, 2) == half), col_id * 8 + vec, -1)
    strip = lax.broadcasted_iota(jnp.int32, (16, SLOTS * 16), 0)

    def fill_f(i, carry):
        hot_f[pl.ds(pl.multiple_of(i * 16, 16), 16), :] = jnp.where(strip + i * 16 == key_f, 1.0, 0.0).astype(BF16)
        return carry

    def fill_b(i, carry):
        hot_b[pl.ds(pl.multiple_of(i * 16, 16), 16), :] = jnp.where(strip + i * 16 == key_b, 1.0, 0.0).astype(BF16)
        return carry

    lax.fori_loop(0, 16, fill_f, 0)
    lax.fori_loop(0, 32, fill_b, 0)
    for i in (4, 5, 6, 8):
        loads[i].wait()

    pl.semaphore_wait(barrier, 46)

    def send_gather(k):
        base = 8 * k
        each_line(lambda other, device: send(rowx[k].at[c], rowx[k].at[c], base, device))
        send(colx[k].at[r], colx[k].at[r], base + 1, partner)
        each_plane(lambda other, device: send(colx[k].at[r], colx[k].at[r], base + 2, device))

    def forward_partner(k):
        base = 8 * k
        arrived(base + 1, colx[k].at[mate])
        each_plane(lambda other, device: send(colx[k].at[mate], colx[k].at[mate], base + 3, device))

    def products(index, source, dims):
        def step(i, carry):
            for u in range(UNROLL):
                t = i * UNROLL + u
                block = source[lax.div(index[0, 0, t], 2)]
                out = lax.dot_general(block, tiles[0, 0, t], dims, preferred_element_type=F32)
                prod[pl.ds(pl.multiple_of(t * 16, 16), 16), :] = out.astype(BF16)
            return carry

        lax.fori_loop(0, SLOTS // UNROLL, step, 0)

    def to_columns(out):
        for g in range(4):
            part = jnp.dot(hot_b[pl.ds(g * 128, 128), :], prod[...], preferred_element_type=F32)
            out[pl.ds(g * 4, 4)] = part.astype(BF16).reshape(4, 32, 128)

    def transposed_part(k):
        base = 8 * k
        arrived(base, rowx[k].at[pl.ds(0, 15)])
        products(rows_s, rowx[k], NN)
        to_columns(col_send.at[k])
        col_recv[k, q] = col_send[k, q]
        each_plane(lambda other, device: send(col_send.at[k, other], col_recv.at[k, q], base + 4, device))

    def forward_part(k):
        base = 8 * k
        arrived(base + 2, colx[k].at[pl.ds(0, 15)])
        arrived(base + 3, colx[k].at[pl.ds(0, 15)])
        products(cols_s, colx[k], NT)
        for g in range(2):
            part = jnp.dot(hot_f[pl.ds(g * 128, 128), :], prod[...], preferred_element_type=F32)
            row_send[k, pl.ds(g * 8, 8)] = part.astype(BF16).reshape(8, 16, 128)
        row_recv[k, c] = row_send[k, c]
        each_line(lambda other, device: send(row_send.at[k, other], row_recv.at[k, c], base + 5, device))

    def total(ref, n):
        out = ref[0].astype(F32)
        for i in range(1, n):
            out = out + ref[i].astype(F32)
        return out

    def split(both):
        return jnp.where(zh == 0, both[:16], both[16:]), jnp.where(zh == 0, both[16:], both[:16])

    def column_sums(k):
        base = 8 * k
        arrived(base + 4, col_recv.at[k, pl.ds(0, 15)])
        mine, theirs = split(total(col_recv.at[k], 16))
        part_send[k] = theirs
        send(part_send.at[k], part_recv.at[k], base + 6, partner)
        return mine, theirs

    def finish(k, mine):
        base = 8 * k
        arrived(base + 5, row_recv.at[k, pl.ds(0, 15)])
        out = mine + total(row_recv.at[k], 16)
        arrived(base + 6, part_recv.at[k])
        return out + part_recv[k]

    send_gather(0)
    send(xv, partner_x, 16, partner)
    stack[0:8] = xv[...]
    stack[16:24] = pv[...]
    images[24:32] = hpv[...]
    transposed_part(0)
    forward_partner(0)
    send(pv, partner_p, 24, partner)
    each_line(lambda other, device: send(rowp.at[c], rowp.at[c], 25, device))
    mine, theirs = column_sums(0)

    arrived(16, partner_x)
    weighted = x_tall * mine + fold(partner_x[...]) * theirs
    squared = x_tall * x_tall
    num = jnp.sum(weighted[:8] + weighted[8:], axis=1, keepdims=True)
    den = jnp.sum(squared[:8] + squared[8:], axis=1, keepdims=True)
    sub8 = lax.broadcasted_iota(jnp.int32, (8, 128), 0)
    lane8 = lax.broadcasted_iota(jnp.int32, (8, 128), 1)
    placed = jnp.where(lane8 == sub8, num, jnp.where(lane8 == sub8 + 8, den, 0.0))
    th1[q] = jnp.sum(placed, axis=0, keepdims=True)
    each_plane(lambda other, device: send(th1.at[q], th1.at[q], 17, device))
    forward_part(0)
    arrived(17, th1.at[pl.ds(0, 15)])
    acc = total(th1, 16)
    th2[zslot] = acc
    each_ring(lambda device: send(th2.at[zslot], th2.at[zslot], 18, device))

    arrived(25, rowp.at[pl.ds(0, 15)])
    products(rows_s, rowp, NN)
    to_columns(colp_send)
    colp_recv[q] = colp_send[q]
    each_plane(lambda other, device: send(colp_send.at[other], colp_recv.at[q], 26, device))

    hx_tall = finish(0, mine)
    arrived(18, th2.at[pl.ds(0, 31)])
    acc = total(th2, 32)
    num = 2.0 * jnp.sum(jnp.where(lane8 == sub8, acc, 0.0), axis=1, keepdims=True)
    den = jnp.sum(jnp.where(lane8 == sub8 + 8, acc, 0.0), axis=1, keepdims=True)
    theta = num / den
    theta_tall = jnp.concatenate([theta, theta], axis=0)
    res_tall = hx_tall - theta_tall * x_tall
    res_round = res_tall.astype(BF16)
    rowx[1][c] = res_round
    colx[1][r] = res_round

    send_gather(1)
    residual = unfold(res_tall)
    res_out[...] = residual
    stack[8:16] = residual
    stack[24:32] = unfold(hx_tall)
    images[0:24] = stack[0:24]
    images[32:40] = stack[24:32]
    images[40:48] = unfold(res_round.astype(F32))
    early = exact(stack[...], images[...])
    early = jnp.concatenate([early, jnp.zeros((32, 80), F32)], axis=1)
    for i in range(16):
        early_send[i] = early[2 * i : 2 * i + 2]
    early1[q] = early_send[q]
    each_plane(lambda other, device: send(early_send.at[other], early1.at[q], 19, device))
    transposed_part(1)
    forward_partner(1)
    arrived(19, early1.at[pl.ds(0, 15)])
    acc = total(early1, 16)
    early2[zslot] = acc
    each_ring(lambda device: send(early2.at[zslot], early2.at[zslot], 20, device))

    arrived(26, colp_recv.at[pl.ds(0, 15)])
    arrived(24, partner_p)
    res_pair = jnp.concatenate([unfold(res_round.astype(F32)), unfold(colx[1][mate].astype(F32))], axis=1)
    p_pair = jnp.concatenate([pv[...], partner_p[...]], axis=1)
    hp_mine, hp_theirs = split(total(colp_recv, 16))
    hp_pair = jnp.concatenate([unfold(hp_mine), unfold(hp_theirs)], axis=1)
    other_side = jnp.concatenate([jnp.zeros((8, 8), F32), exact(hp_pair, res_pair)], axis=0)
    sides = jnp.concatenate([res_pair, p_pair], axis=0)
    mine, theirs = column_sums(1)
    pair = jnp.concatenate([unfold(mine), unfold(theirs)], axis=1)
    late = exact(sides, pair) + other_side
    late = jnp.concatenate([late, jnp.zeros((16, 120), F32)], axis=1)
    late1[q] = jnp.sum(pltpu.roll(late, 0, 1, stride=8, stride_axis=0), axis=0, keepdims=True)
    each_plane(lambda other, device: send(late1.at[q], late1.at[q], 22, device))
    forward_part(1)

    arrived(22, late1.at[pl.ds(0, 15)])
    late2[zslot] = total(late1, 16)
    each_ring(lambda device: send(late2.at[zslot], late2.at[zslot], 23, device))
    arrived(20, early2.at[pl.ds(0, 31)])
    early3[q] = total(early2, 32)
    each_plane(lambda other, device: send(early3.at[q], early3.at[q], 21, device))

    img_out[...] = unfold(finish(1, mine))
    cells = 1.0 / 131072.0
    from_lane = lax.broadcasted_iota(jnp.int32, (128, 256), 1)
    from_vec = jnp.where(from_lane < 128, lax.rem(from_lane, 8), lax.div(from_lane - 128, 8))
    place = jnp.where(lax.broadcasted_iota(jnp.int32, (128, 256), 0) == 8 + from_vec, 1.0, 0.0)
    at = lax.broadcasted_iota(jnp.int32, (16, 256), 1)
    at_row = lax.broadcasted_iota(jnp.int32, (16, 256), 0)
    source = jnp.where(at < 128, lax.div(at, 8), jnp.where((at < 192) & (at_row < 8), lax.rem(at, 8), -1))
    arrived(21, early3.at[pl.ds(0, 15)])
    early = jnp.concatenate([early3[i] for i in range(16)], axis=0) * cells
    gs_out[...] = early[:24, :24]
    hx_part = pltpu.roll(early[:24], 128 - 32, 1)
    hp_part = pltpu.roll(early[:24], 128 - 8, 1)
    image_x = pltpu.roll(early[24:32], 128 - 32, 1)

    arrived(23, late2.at[pl.ds(0, 31)])
    late = total(late2, 32) * cells
    late = exact(jnp.where(source == at_row, jnp.concatenate([late, late], axis=1), 0.0), place)
    image_part = jnp.concatenate([image_x, late], axis=0)
    lane24 = lax.broadcasted_iota(jnp.int32, (24, 128), 1)
    whole = jnp.where(lane24 < 8, hx_part, jnp.where(lane24 < 16, image_part, hp_part))
    gh_out[...] = whole[:, :24]

    for which, ref in sent:
        wait_on(send_sem.at[which], ref)


def deliver(a, b, c, d, out_a, out_b, out_c, out_d, sem):
    pairs = ((a, out_a), (b, out_b), (c, out_c), (d, out_d))
    copies = [pltpu.make_async_copy(src, dst, sem.at[i]) for i, (src, dst) in enumerate(pairs)]
    for copy in copies:
        copy.start()
    for copy in copies:
        copy.wait()


def solution(mesh):
    def body(x_block, p_block, hp_block, tile_rows, tile_cols, tile_count, tile_values):
        any_spec = pl.BlockSpec(memory_space=pl.ANY)
        hbm = pl.BlockSpec(memory_space=pltpu.HBM)
        vmem = pl.BlockSpec(memory_space=pltpu.VMEM)
        shapes = (
            jax.ShapeDtypeStruct((8, 256), F32),
            jax.ShapeDtypeStruct((8, 256), F32),
            jax.ShapeDtypeStruct((24, 24), F32),
            jax.ShapeDtypeStruct((24, 24), F32),
        )
        results = pl.pallas_call(
            kernel,
            out_shape=shapes,
            in_specs=[any_spec] * 7,
            out_specs=(vmem,) * 4,
            scratch_shapes=[
                pltpu.VMEM((8, 256), F32), pltpu.VMEM((8, 256), F32), pltpu.VMEM((8, 256), F32),
                pltpu.VMEM((1, 1, SLOTS), jnp.int32), pltpu.VMEM((1, 1, SLOTS), jnp.int32),
                pltpu.SMEM((1, 1, SLOTS), jnp.int32), pltpu.SMEM((1, 1, SLOTS), jnp.int32),
                pltpu.SMEM((1, 1), jnp.int32),
                pltpu.VMEM((1, 1, SLOTS, 128, 128), BF16),
                pltpu.VMEM((256, SLOTS * 16), BF16), pltpu.VMEM((512, SLOTS * 16), BF16),
                pltpu.VMEM((SLOTS * 16, 128), BF16),
                pltpu.VMEM((16, 16, 128), BF16), pltpu.VMEM((16, 16, 128), BF16),
                pltpu.VMEM((32, 16, 128), BF16), pltpu.VMEM((32, 16, 128), BF16),
                pltpu.VMEM((2, 16, 16, 128), BF16), pltpu.VMEM((2, 16, 16, 128), BF16),
                pltpu.VMEM((2, 16, 32, 128), BF16), pltpu.VMEM((2, 16, 32, 128), BF16),
                pltpu.VMEM((2, 16, 128), F32), pltpu.VMEM((2, 16, 128), F32),
                pltpu.VMEM((32, 256), F32), pltpu.VMEM((48, 256), F32),
                pltpu.VMEM((8, 256), F32), pltpu.VMEM((8, 256), F32),
                pltpu.VMEM((16, 16, 128), BF16), pltpu.VMEM((16, 32, 128), BF16), pltpu.VMEM((16, 32, 128), BF16),
                pltpu.VMEM((16, 1, 128), F32), pltpu.VMEM((32, 1, 128), F32),
                pltpu.VMEM((16, 2, 128), F32), pltpu.VMEM((16, 2, 128), F32),
                pltpu.VMEM((32, 2, 128), F32), pltpu.VMEM((16, 2, 128), F32),
                pltpu.VMEM((16, 1, 128), F32), pltpu.VMEM((32, 1, 128), F32),
                pltpu.SemaphoreType.DMA((9,)), pltpu.SemaphoreType.DMA((27,)), pltpu.SemaphoreType.DMA((27,)),
            ],
            compiler_params=pltpu.CompilerParams(
                collective_id=0, has_side_effects=True, vmem_limit_bytes=VMEM_LIMIT
            ),
        )(*[pltpu.with_memory_space_constraint(v, pltpu.HBM) for v in (x_block, p_block, hp_block, tile_rows, tile_cols)], tile_count, pltpu.with_memory_space_constraint(tile_values, pltpu.HBM))
        return pl.pallas_call(
            deliver,
            out_shape=shapes,
            in_specs=[any_spec] * 4,
            out_specs=(any_spec,) * 4,
            scratch_shapes=[pltpu.SemaphoreType.DMA((4,))],
        )(*[pltpu.with_memory_space_constraint(v, pltpu.VMEM) for v in results])

    in_specs = (
        P(None, ("row", "col")),
        P(None, ("row", "col")),
        P(None, ("row", "col")),
        P("row", "col", None),
        P("row", "col", None),
        P("row", "col"),
        P("row", "col", None, None, None),
    )
    out_specs = (P(None, ("row", "col")), P(None, ("row", "col")), P(), P())
    return jax.shard_map(body, mesh=mesh, in_specs=in_specs, out_specs=out_specs, check_vma=False)
```

```python
import jax
import jax.numpy as jnp
from jax import lax
from jax.experimental import pallas as pl
from jax.experimental.pallas import tpu as pltpu
from jax.sharding import PartitionSpec as P

MESH = pl.DeviceIdType.MESH
F32 = jnp.float32
BF16 = jnp.bfloat16
SLOTS = 48
VMEM_LIMIT = 32 * 1024 * 1024
NT = (((1,), (1,)), ((), ()))
def kernel(
    x_hbm, p_hbm, hp_hbm, rows_hbm, cols_hbm, count_hbm, tiles_hbm,
    res_out, img_out, gs_out, gh_out,
    xv, pv, hpv, rows_v, cols_v, rows_s, cols_s, count_s, tiles,
    hot_f, hot_b, prod, rowx0, rowx1, colx0, colx1, row_send, row_recv, col_send, col_recv,
    part_send, part_recv, stack, images, partner_x, partner_p, rowp, colp_send, colp_recv,
    th1, th2, early_send, early1, early2, early3, late1, late2,
    local_sem, send_sem, recv_sem,
):
    rowx, colx = (rowx0, rowx1), (colx0, colx1)
    r = lax.axis_index("row")
    c = lax.axis_index("col")
    zh = lax.rem(r, 2)
    q = lax.div(r, 2)
    y, xx = lax.div(q, 4), lax.rem(q, 4)
    core = lax.rem(c, 2)
    z = zh * 8 + lax.div(c, 2)
    mate = r + 1 - 2 * zh
    partner = (mate, c)
    spot = q * 2 + core

    def each_plane(act):
        def step(i, carry):
            a, b = lax.div(i, 4), lax.rem(i, 4)
            dy = jnp.where(a < 2, 2 - a, 9 - 3 * a)
            dx = jnp.where(b < 2, 2 - b, 9 - 3 * b)
            other = lax.rem(y + dy, 4) * 4 + lax.rem(xx + dx, 4)
            act(other, (other * 2 + zh, c))
            return carry

        lax.fori_loop(0, 15, step, 0)

    def each_line(act):
        def step(i, carry):
            down = 15 - i - jnp.where(15 - i <= c, 1, 0)
            up = i + jnp.where(i >= c, 1, 0)
            other = jnp.where(c < 8, down, up)
            act(other, (r, other))
            return carry

        lax.fori_loop(0, 15, step, 0)

    def each_pole(act):
        def step(i, carry):
            s = lax.div(i + 1, 2)
            oz = lax.rem(z + 8 + jnp.where(lax.rem(i, 2) == 0, s, -s), 16)
            act((q * 2 + lax.div(oz, 8), lax.rem(oz, 8) * 2 + core))
            return carry

        lax.fori_loop(0, 15, step, 0)

    def each_disc(act):
        def step(i, carry):
            m = lax.div(i, 2)
            a, b = lax.div(m, 4), lax.rem(m, 4)
            dy = jnp.where(a < 2, 2 - a, 9 - 3 * a)
            dx = jnp.where(b < 2, 2 - b, 9 - 3 * b)
            other = lax.rem(y + dy, 4) * 4 + lax.rem(xx + dx, 4)
            k = jnp.where(m == 15, 1 - core, lax.rem(i, 2))
            act(other * 2 + k, (other * 2 + zh, c - core + k))
            return carry

        lax.fori_loop(0, 31, step, 0)

    def each_far_pole(act):
        def step(i, carry):
            act((mate, 2 * i + core))
            return carry

        lax.fori_loop(0, 8, step, 0)

    loads = [
        pltpu.make_async_copy(src, dst, local_sem.at[i])
        for i, (src, dst) in enumerate(
            [
                (x_hbm, xv), (rows_hbm, rows_v), (cols_hbm, cols_v), (count_hbm, count_s),
                (rows_hbm, rows_s), (cols_hbm, cols_s), (tiles_hbm, tiles), (p_hbm, pv), (hp_hbm, hpv),
            ]
        )
    ]
    loads[0].start()
    barrier = pltpu.get_barrier_semaphore()

    def greet(device):
        pl.semaphore_signal(barrier, inc=1, device_id=device, device_id_type=MESH)

    each_far_pole(greet)
    each_line(lambda other, device: greet(device))
    each_disc(lambda other, device: greet(device))

    for load in loads[1:]:
        load.start()

    def send(src, dst, which, device):
        pltpu.make_async_remote_copy(
            src_ref=src, dst_ref=dst, send_sem=send_sem.at[which], recv_sem=recv_sem.at[which],
            device_id=device, device_id_type=MESH,
        ).start()

    def wait_on(sem, ref):
        pltpu.make_async_copy(ref, ref, sem).wait()

    sent = []

    def arrived(which, ref):
        wait_on(recv_sem.at[which], ref)
        sent.append((which, ref))

    def exact(a, b):
        return lax.dot_general(a, b, NT, precision=lax.Precision.HIGHEST, preferred_element_type=F32)

    def fold(wide):
        return jnp.concatenate([wide[:, :128], wide[:, 128:]], axis=0)

    def unfold(tall):
        return jnp.concatenate([tall[:8], tall[8:]], axis=1)

    loads[0].wait()
    x_tall = fold(xv[...])
    x_round = x_tall.astype(BF16)
    rowx[0][c] = x_round
    colx[0][r] = x_round

    pl.semaphore_wait(barrier, 54)

    def send_gather(k):
        base = 8 * k
        each_line(lambda other, device: send(rowx[k].at[c], rowx[k].at[c], base, device))
        send(colx[k].at[r], colx[k].at[r], base + 1, partner)
        each_plane(lambda other, device: send(colx[k].at[r], colx[k].at[r], base + 2, device))

    def forward_partner(k):
        base = 8 * k
        arrived(base + 1, colx[k].at[mate])
        each_plane(lambda other, device: send(colx[k].at[mate], colx[k].at[mate], base + 3, device))

    def products(index, source, dims):
        for t in range(SLOTS):
            block = source[lax.div(index[0, 0, t], 2)]
            out = lax.dot_general(block, tiles[0, 0, t], dims, preferred_element_type=F32)
            prod[16 * t : 16 * t + 16, :] = out.astype(BF16)

    def paired_products(source):
        none = jnp.zeros((16, 128), BF16)
        for t in range(0, SLOTS, 2):
            upper = jnp.concatenate([source[lax.div(rows_s[0, 0, t], 2)], none], axis=1)
            lower = jnp.concatenate([none, source[lax.div(rows_s[0, 0, t + 1], 2)]], axis=1)
            out = jnp.dot(
                jnp.concatenate([upper, lower], axis=0),
                tiles[0, 0, t : t + 2].reshape(256, 128),
                preferred_element_type=F32,
            )
            prod[16 * t : 16 * t + 32, :] = out.astype(BF16)

    def to_columns(out, landing, which):
        for step in range(4):
            g = lax.rem(y + (2, 1, 3, 0)[step], 4)
            rows = pl.ds(pl.multiple_of(g * 128, 128), 128)
            part = jnp.dot(hot_b[rows, :], prod[...], preferred_element_type=F32)
            out[pl.ds(g * 4, 4)] = part.astype(BF16).reshape(4, 32, 128)
            if step == 3:
                landing[q] = out[q]

            def give(i, carry):
                other = g * 4 + lax.rem(xx + jnp.where(i < 2, 2 - i, 9 - 3 * i), 4)
                send(out.at[other], landing.at[q], which, (other * 2 + zh, c))
                return carry

            lax.fori_loop(0, 3 if step == 3 else 4, give, 0)

    def transposed_part(k):
        base = 8 * k
        arrived(base, rowx[k].at[pl.ds(0, 15)])
        paired_products(rowx[k])
        to_columns(col_send.at[k], col_recv.at[k], base + 4)

    def forward_part(k):
        base = 8 * k
        arrived(base + 2, colx[k].at[pl.ds(0, 15)])
        arrived(base + 3, colx[k].at[pl.ds(0, 15)])
        products(cols_s, colx[k], NT)
        for g in range(2):
            part = jnp.dot(hot_f[pl.ds(g * 128, 128), :], prod[...], preferred_element_type=F32)
            row_send[k, pl.ds(g * 8, 8)] = part.astype(BF16).reshape(8, 16, 128)
        row_recv[k, c] = row_send[k, c]
        each_line(lambda other, device: send(row_send.at[k, other], row_recv.at[k, c], base + 5, device))

    def total(ref, n):
        terms = [ref[i].astype(F32) for i in range(n)]
        while len(terms) > 1:
            terms = [a + b for a, b in zip(terms[::2], terms[1::2], strict=True)]
        return terms[0]

    def split(both):
        return jnp.where(zh == 0, both[:16], both[16:]), jnp.where(zh == 0, both[16:], both[:16])

    def column_sums(k):
        base = 8 * k
        arrived(base + 4, col_recv.at[k, pl.ds(0, 15)])
        mine, theirs = split(total(col_recv.at[k], 16))
        part_send[k] = theirs
        send(part_send.at[k], part_recv.at[k], base + 6, partner)
        return mine, theirs

    def finish(k, mine):
        base = 8 * k
        arrived(base + 5, row_recv.at[k, pl.ds(0, 15)])
        out = mine + total(row_recv.at[k], 16)
        arrived(base + 6, part_recv.at[k])
        return out + part_recv[k]

    send_gather(0)
    send(xv, partner_x, 16, partner)
    for i in (1, 2, 3):
        loads[i].wait()
    sub = lax.broadcasted_iota(jnp.int32, (16, SLOTS), 0)
    lane = lax.broadcasted_iota(jnp.int32, (16, SLOTS), 1)
    alive = jnp.where(lane < count_s[0, 0], 1.0, 0.0)
    table = jnp.where(
        sub == 0, rows_v[0].astype(F32), jnp.where(sub == 1, cols_v[0].astype(F32), alive)
    ).astype(BF16)
    spread = jnp.where(
        lax.div(lax.broadcasted_iota(jnp.int32, (SLOTS, SLOTS * 16), 1), 16)
        == lax.broadcasted_iota(jnp.int32, (SLOTS, SLOTS * 16), 0),
        1.0, 0.0,
    ).astype(BF16)
    wide = jnp.dot(table, spread, preferred_element_type=F32).astype(jnp.int32)
    row_id, col_id, on = wide[0:1], wide[1:2], wide[2:3]
    pos = lax.broadcasted_iota(jnp.int32, (1, SLOTS * 16), 1)
    vec = lax.rem(pos, 8)
    half = lax.rem(lax.div(pos, 8), 2)
    key_f = jnp.where((on == 1) & (lax.rem(col_id, 2) == half), row_id * 8 + vec, -1)
    key_b = jnp.where((on == 1) & (lax.rem(row_id, 2) == half), col_id * 8 + vec, -1)
    strip = lax.broadcasted_iota(jnp.int32, (16, SLOTS * 16), 0)

    def fill_f(i, carry):
        hot_f[pl.ds(pl.multiple_of(i * 16, 16), 16), :] = jnp.where(strip + i * 16 == key_f, 1.0, 0.0).astype(BF16)
        return carry

    def fill_b(i, carry):
        hot_b[pl.ds(pl.multiple_of(i * 16, 16), 16), :] = jnp.where(strip + i * 16 == key_b, 1.0, 0.0).astype(BF16)
        return carry

    lax.fori_loop(0, 16, fill_f, 0)
    lax.fori_loop(0, 32, fill_b, 0)
    for i in (4, 5, 6, 8):
        loads[i].wait()

    loads[7].wait()
    rowp[c] = fold(pv[...]).astype(BF16)
    stack[0:8] = xv[...]
    stack[16:24] = pv[...]
    images[24:32] = hpv[...]
    transposed_part(0)
    forward_partner(0)
    send(pv, partner_p, 24, partner)
    each_line(lambda other, device: send(rowp.at[c], rowp.at[c], 25, device))
    mine, theirs = column_sums(0)

    arrived(16, partner_x)
    weighted = x_tall * mine + fold(partner_x[...]) * theirs
    squared = x_tall * x_tall
    num = jnp.sum(weighted[:8] + weighted[8:], axis=1, keepdims=True)
    den = jnp.sum(squared[:8] + squared[8:], axis=1, keepdims=True)
    sub8 = lax.broadcasted_iota(jnp.int32, (8, 128), 0)
    lane8 = lax.broadcasted_iota(jnp.int32, (8, 128), 1)
    placed = jnp.where(lane8 == sub8, num, jnp.where(lane8 == sub8 + 8, den, 0.0))
    th1[spot] = jnp.sum(placed, axis=0, keepdims=True)
    each_disc(lambda other, device: send(th1.at[spot], th1.at[spot], 17, device))
    forward_part(0)
    arrived(17, th1.at[pl.ds(0, 31)])
    acc = total(th1, 32)
    th2[z] = acc
    each_pole(lambda device: send(th2.at[z], th2.at[z], 18, device))

    arrived(25, rowp.at[pl.ds(0, 15)])
    paired_products(rowp)
    to_columns(colp_send, colp_recv, 26)

    hx_tall = finish(0, mine)
    arrived(18, th2.at[pl.ds(0, 15)])
    acc = total(th2, 16)
    num = 2.0 * jnp.sum(jnp.where(lane8 == sub8, acc, 0.0), axis=1, keepdims=True)
    den = jnp.sum(jnp.where(lane8 == sub8 + 8, acc, 0.0), axis=1, keepdims=True)
    theta = num / den
    theta_tall = jnp.concatenate([theta, theta], axis=0)
    res_tall = hx_tall - theta_tall * x_tall
    res_round = res_tall.astype(BF16)
    rowx[1][c] = res_round
    colx[1][r] = res_round

    send_gather(1)
    residual = unfold(res_tall)
    res_out[...] = residual
    stack[8:16] = residual
    stack[24:32] = unfold(hx_tall)
    images[0:24] = stack[0:24]
    images[32:40] = stack[24:32]
    images[40:48] = unfold(res_round.astype(F32))
    early = exact(stack[...], images[...])
    early = jnp.concatenate([early, jnp.zeros((32, 80), F32)], axis=1)
    for i in range(32):
        early_send[i] = early[i : i + 1]
    early1[spot] = early_send[spot]
    each_disc(lambda other, device: send(early_send.at[other], early1.at[spot], 19, device))
    transposed_part(1)
    forward_partner(1)
    arrived(19, early1.at[pl.ds(0, 31)])
    acc = total(early1, 32)
    early2[z] = acc
    each_pole(lambda device: send(early2.at[z], early2.at[z], 20, device))

    arrived(26, colp_recv.at[pl.ds(0, 15)])
    arrived(24, partner_p)
    res_pair = jnp.concatenate([unfold(res_round.astype(F32)), unfold(colx[1][mate].astype(F32))], axis=1)
    p_pair = jnp.concatenate([pv[...], partner_p[...]], axis=1)
    hp_mine, hp_theirs = split(total(colp_recv, 16))
    hp_pair = jnp.concatenate([unfold(hp_mine), unfold(hp_theirs)], axis=1)
    other_side = jnp.concatenate([jnp.zeros((8, 8), F32), exact(hp_pair, res_pair)], axis=0)
    p_high = p_pair.astype(BF16).astype(F32)
    sides = jnp.concatenate([res_pair, p_high, p_pair - p_high], axis=0).astype(BF16)
    mine, theirs = column_sums(1)
    pair = jnp.concatenate([unfold(mine), unfold(theirs)], axis=1)
    high = pair.astype(BF16)
    low = (pair - high.astype(F32)).astype(BF16)
    late = lax.dot_general(sides, high, NT, preferred_element_type=F32)
    late = late + lax.dot_general(sides, low, NT, preferred_element_type=F32)
    late = late[0:16] + jnp.concatenate([jnp.zeros((8, 8), F32), late[16:24]], axis=0) + other_side
    late = jnp.concatenate([late, jnp.zeros((16, 120), F32)], axis=1)
    late1[spot] = jnp.sum(pltpu.roll(late, 0, 1, stride=8, stride_axis=0), axis=0, keepdims=True)
    each_disc(lambda other, device: send(late1.at[spot], late1.at[spot], 22, device))
    forward_part(1)

    arrived(22, late1.at[pl.ds(0, 31)])
    late2[z] = total(late1, 32)
    each_pole(lambda device: send(late2.at[z], late2.at[z], 23, device))
    arrived(20, early2.at[pl.ds(0, 15)])
    early3[spot] = total(early2, 16)
    each_disc(lambda other, device: send(early3.at[spot], early3.at[spot], 21, device))

    img_out[...] = unfold(finish(1, mine))
    cells = 1.0 / 131072.0
    from_lane = lax.broadcasted_iota(jnp.int32, (128, 256), 1)
    from_vec = jnp.where(from_lane < 128, lax.rem(from_lane, 8), lax.div(from_lane - 128, 8))
    place = jnp.where(lax.broadcasted_iota(jnp.int32, (128, 256), 0) == 8 + from_vec, 1.0, 0.0)
    at = lax.broadcasted_iota(jnp.int32, (16, 256), 1)
    at_row = lax.broadcasted_iota(jnp.int32, (16, 256), 0)
    source = jnp.where(at < 128, lax.div(at, 8), jnp.where((at < 192) & (at_row < 8), lax.rem(at, 8), -1))
    arrived(21, early3.at[pl.ds(0, 31)])
    early = jnp.concatenate([early3[i] for i in range(32)], axis=0) * cells
    gs_out[...] = early[:24, :24]
    hx_part = pltpu.roll(early[:24], 128 - 32, 1)
    hp_part = pltpu.roll(early[:24], 128 - 8, 1)
    image_x = pltpu.roll(early[24:32], 128 - 32, 1)

    arrived(23, late2.at[pl.ds(0, 15)])
    late = total(late2, 16) * cells
    parts, rest = [], late
    for _ in range(3):
        part = rest.astype(BF16).astype(F32)
        rest = rest - part
        parts.append(jnp.where(source == at_row, jnp.concatenate([part, part], axis=1), 0.0))
    late = lax.dot_general(
        jnp.concatenate(parts, axis=0).astype(BF16), place.astype(BF16), NT, preferred_element_type=F32
    )
    late = late[0:16] + late[16:32] + late[32:48]
    image_part = jnp.concatenate([image_x, late], axis=0)
    lane24 = lax.broadcasted_iota(jnp.int32, (24, 128), 1)
    whole = jnp.where(lane24 < 8, hx_part, jnp.where(lane24 < 16, image_part, hp_part))
    gh_out[...] = whole[:, :24]

    for which, ref in sent:
        wait_on(send_sem.at[which], ref)


def deliver(a, b, c, d, out_a, out_b, out_c, out_d, sem):
    pairs = ((a, out_a), (b, out_b), (c, out_c), (d, out_d))
    copies = [pltpu.make_async_copy(src, dst, sem.at[i]) for i, (src, dst) in enumerate(pairs)]
    for copy in copies:
        copy.start()
    for copy in copies:
        copy.wait()


def solution(mesh):
    def body(x_block, p_block, hp_block, tile_rows, tile_cols, tile_count, tile_values):
        any_spec = pl.BlockSpec(memory_space=pl.ANY)
        hbm = pl.BlockSpec(memory_space=pltpu.HBM)
        vmem = pl.BlockSpec(memory_space=pltpu.VMEM)
        shapes = (
            jax.ShapeDtypeStruct((8, 256), F32),
            jax.ShapeDtypeStruct((8, 256), F32),
            jax.ShapeDtypeStruct((24, 24), F32),
            jax.ShapeDtypeStruct((24, 24), F32),
        )
        results = pl.pallas_call(
            kernel,
            out_shape=shapes,
            in_specs=[any_spec] * 7,
            out_specs=(vmem,) * 4,
            scratch_shapes=[
                pltpu.VMEM((8, 256), F32), pltpu.VMEM((8, 256), F32), pltpu.VMEM((8, 256), F32),
                pltpu.VMEM((1, 1, SLOTS), jnp.int32), pltpu.VMEM((1, 1, SLOTS), jnp.int32),
                pltpu.SMEM((1, 1, SLOTS), jnp.int32), pltpu.SMEM((1, 1, SLOTS), jnp.int32),
                pltpu.SMEM((1, 1), jnp.int32),
                pltpu.VMEM((1, 1, SLOTS, 128, 128), BF16),
                pltpu.VMEM((256, SLOTS * 16), BF16), pltpu.VMEM((512, SLOTS * 16), BF16),
                pltpu.VMEM((SLOTS * 16, 128), BF16),
                pltpu.VMEM((16, 16, 128), BF16), pltpu.VMEM((16, 16, 128), BF16),
                pltpu.VMEM((32, 16, 128), BF16), pltpu.VMEM((32, 16, 128), BF16),
                pltpu.VMEM((2, 16, 16, 128), BF16), pltpu.VMEM((2, 16, 16, 128), BF16),
                pltpu.VMEM((2, 16, 32, 128), BF16), pltpu.VMEM((2, 16, 32, 128), BF16),
                pltpu.VMEM((2, 16, 128), F32), pltpu.VMEM((2, 16, 128), F32),
                pltpu.VMEM((32, 256), F32), pltpu.VMEM((48, 256), F32),
                pltpu.VMEM((8, 256), F32), pltpu.VMEM((8, 256), F32),
                pltpu.VMEM((16, 16, 128), BF16), pltpu.VMEM((16, 32, 128), BF16), pltpu.VMEM((16, 32, 128), BF16),
                pltpu.VMEM((32, 1, 128), F32), pltpu.VMEM((16, 1, 128), F32),
                pltpu.VMEM((32, 1, 128), F32), pltpu.VMEM((32, 1, 128), F32),
                pltpu.VMEM((16, 1, 128), F32), pltpu.VMEM((32, 1, 128), F32),
                pltpu.VMEM((32, 1, 128), F32), pltpu.VMEM((16, 1, 128), F32),
                pltpu.SemaphoreType.DMA((9,)), pltpu.SemaphoreType.DMA((27,)), pltpu.SemaphoreType.DMA((27,)),
            ],
            compiler_params=pltpu.CompilerParams(
                collective_id=0, has_side_effects=True, vmem_limit_bytes=VMEM_LIMIT
            ),
        )(*[pltpu.with_memory_space_constraint(v, pltpu.HBM) for v in (x_block, p_block, hp_block, tile_rows, tile_cols)], tile_count, pltpu.with_memory_space_constraint(tile_values, pltpu.HBM))
        return pl.pallas_call(
            deliver,
            out_shape=shapes,
            in_specs=[any_spec] * 4,
            out_specs=(any_spec,) * 4,
            scratch_shapes=[pltpu.SemaphoreType.DMA((4,))],
        )(*[pltpu.with_memory_space_constraint(v, pltpu.VMEM) for v in results])

    in_specs = (
        P(None, ("row", "col")),
        P(None, ("row", "col")),
        P(None, ("row", "col")),
        P("row", "col", None),
        P("row", "col", None),
        P("row", "col"),
        P("row", "col", None, None, None),
    )
    out_specs = (P(None, ("row", "col")), P(None, ("row", "col")), P(), P())
    return jax.shard_map(body, mesh=mesh, in_specs=in_specs, out_specs=out_specs, check_vma=False)
```

```python
import jax
import jax.numpy as jnp
from jax import lax
from jax.experimental import pallas as pl
from jax.experimental.pallas import tpu as pltpu
from jax.sharding import PartitionSpec as P

MESH = pl.DeviceIdType.MESH
F32 = jnp.float32
BF16 = jnp.bfloat16
SLOTS = 48
VMEM_LIMIT = 32 * 1024 * 1024
NT = (((1,), (1,)), ((), ()))
def kernel(
    x_hbm, p_hbm, hp_hbm, rows_hbm, cols_hbm, count_hbm, tiles_hbm,
    res_out, img_out, gs_out, gh_out,
    xv, pv, hpv, rows_v, cols_v, rows_s, cols_s, count_s, tiles,
    hot_f, hot_b, prod, rowx0, rowx1, colx0, colx1, row_send, row_recv, col_send, col_recv,
    part_send, part_recv, stack, images, partner_x, partner_p, rowp, colp_send, colp_recv,
    th1, th2, early_send, early1, early2, early3, late1, late2,
    local_sem, send_sem, recv_sem,
):
    rowx, colx = (rowx0, rowx1), (colx0, colx1)
    r = lax.axis_index("row")
    c = lax.axis_index("col")
    zh = lax.rem(r, 2)
    q = lax.div(r, 2)
    y, xx = lax.div(q, 4), lax.rem(q, 4)
    core = lax.rem(c, 2)
    z = zh * 8 + lax.div(c, 2)
    mate = r + 1 - 2 * zh
    partner = (mate, c)
    spot = q * 2 + core

    def each_plane(act):
        def step(i, carry):
            a, b = lax.div(i, 4), lax.rem(i, 4)
            dy = jnp.where(a < 2, 2 - a, 9 - 3 * a)
            dx = jnp.where(b < 2, 2 - b, 9 - 3 * b)
            other = lax.rem(y + dy, 4) * 4 + lax.rem(xx + dx, 4)
            act(other, (other * 2 + zh, c))
            return carry

        lax.fori_loop(0, 15, step, 0)

    def each_line(act):
        def step(i, carry):
            down = 15 - i - jnp.where(15 - i <= c, 1, 0)
            up = i + jnp.where(i >= c, 1, 0)
            other = jnp.where(c < 8, down, up)
            act(other, (r, other))
            return carry

        lax.fori_loop(0, 15, step, 0, unroll=True)

    def each_pole(act):
        def step(i, carry):
            s = lax.div(i + 1, 2)
            oz = lax.rem(z + 8 + jnp.where(lax.rem(i, 2) == 0, s, -s), 16)
            act((q * 2 + lax.div(oz, 8), lax.rem(oz, 8) * 2 + core))
            return carry

        lax.fori_loop(0, 15, step, 0, unroll=True)

    def each_disc(act):
        def step(i, carry):
            m = lax.div(i, 2)
            a, b = lax.div(m, 4), lax.rem(m, 4)
            dy = jnp.where(a < 2, 2 - a, 9 - 3 * a)
            dx = jnp.where(b < 2, 2 - b, 9 - 3 * b)
            other = lax.rem(y + dy, 4) * 4 + lax.rem(xx + dx, 4)
            k = jnp.where(m == 15, 1 - core, lax.rem(i, 2))
            act(other * 2 + k, (other * 2 + zh, c - core + k))
            return carry

        lax.fori_loop(0, 31, step, 0)

    def each_far_pole(act):
        def step(i, carry):
            act((mate, 2 * i + core))
            return carry

        lax.fori_loop(0, 8, step, 0)

    loads = [
        pltpu.make_async_copy(src, dst, local_sem.at[i])
        for i, (src, dst) in enumerate(
            [
                (x_hbm, xv), (rows_hbm, rows_v), (cols_hbm, cols_v), (count_hbm, count_s),
                (rows_hbm, rows_s), (cols_hbm, cols_s), (tiles_hbm, tiles), (p_hbm, pv), (hp_hbm, hpv),
            ]
        )
    ]
    loads[0].start()
    barrier = pltpu.get_barrier_semaphore()

    def greet(device):
        pl.semaphore_signal(barrier, inc=1, device_id=device, device_id_type=MESH)

    each_far_pole(greet)
    each_line(lambda other, device: greet(device))
    each_disc(lambda other, device: greet(device))

    for load in loads[1:]:
        load.start()

    def send(src, dst, which, device):
        pltpu.make_async_remote_copy(
            src_ref=src, dst_ref=dst, send_sem=send_sem.at[which], recv_sem=recv_sem.at[which],
            device_id=device, device_id_type=MESH,
        ).start()

    def wait_on(sem, ref):
        pltpu.make_async_copy(ref, ref, sem).wait()

    sent = []

    def arrived(which, ref):
        wait_on(recv_sem.at[which], ref)
        sent.append((which, ref))

    def exact(a, b):
        return lax.dot_general(a, b, NT, precision=lax.Precision.HIGHEST, preferred_element_type=F32)

    def fold(wide):
        return jnp.concatenate([wide[:, :128], wide[:, 128:]], axis=0)

    def unfold(tall):
        return jnp.concatenate([tall[:8], tall[8:]], axis=1)

    loads[0].wait()
    x_tall = fold(xv[...])
    x_round = x_tall.astype(BF16)
    rowx[0][c] = x_round
    colx[0][r] = x_round

    pl.semaphore_wait(barrier, 54)

    def send_gather(k):
        base = 8 * k
        each_line(lambda other, device: send(rowx[k].at[c], rowx[k].at[c], base, device))
        send(colx[k].at[r], colx[k].at[r], base + 1, partner)
        each_plane(lambda other, device: send(colx[k].at[r], colx[k].at[r], base + 2, device))

    def forward_partner(k):
        base = 8 * k
        arrived(base + 1, colx[k].at[mate])
        each_plane(lambda other, device: send(colx[k].at[mate], colx[k].at[mate], base + 3, device))

    def products(index, source, dims):
        for t in range(SLOTS):
            block = source[lax.div(index[0, 0, t], 2)]
            out = lax.dot_general(block, tiles[0, 0, t], dims, preferred_element_type=F32)
            prod[16 * t : 16 * t + 16, :] = out.astype(BF16)

    def paired_products(source):
        none = jnp.zeros((16, 128), BF16)
        for t in range(0, SLOTS, 2):
            upper = jnp.concatenate([source[lax.div(rows_s[0, 0, t], 2)], none], axis=1)
            lower = jnp.concatenate([none, source[lax.div(rows_s[0, 0, t + 1], 2)]], axis=1)
            out = jnp.dot(
                jnp.concatenate([upper, lower], axis=0),
                tiles[0, 0, t : t + 2].reshape(256, 128),
                preferred_element_type=F32,
            )
            prod[16 * t : 16 * t + 32, :] = out.astype(BF16)

    def to_columns(out, landing, which):
        for step in range(4):
            g = lax.rem(y + (2, 1, 3, 0)[step], 4)
            rows = pl.ds(pl.multiple_of(g * 128, 128), 128)
            part = jnp.dot(hot_b[rows, :], prod[...], preferred_element_type=F32)
            out[pl.ds(g * 4, 4)] = part.astype(BF16).reshape(4, 32, 128)
            if step == 3:
                landing[q] = out[q]

            def give(i, carry):
                other = g * 4 + lax.rem(xx + jnp.where(i < 2, 2 - i, 9 - 3 * i), 4)
                send(out.at[other], landing.at[q], which, (other * 2 + zh, c))
                return carry

            lax.fori_loop(0, 3 if step == 3 else 4, give, 0)

    def transposed_part(k):
        base = 8 * k
        arrived(base, rowx[k].at[pl.ds(0, 15)])
        paired_products(rowx[k])
        to_columns(col_send.at[k], col_recv.at[k], base + 4)

    def forward_part(k):
        base = 8 * k
        arrived(base + 2, colx[k].at[pl.ds(0, 15)])
        arrived(base + 3, colx[k].at[pl.ds(0, 15)])
        products(cols_s, colx[k], NT)
        for g in range(2):
            part = jnp.dot(hot_f[pl.ds(g * 128, 128), :], prod[...], preferred_element_type=F32)
            row_send[k, pl.ds(g * 8, 8)] = part.astype(BF16).reshape(8, 16, 128)
        row_recv[k, c] = row_send[k, c]
        each_line(lambda other, device: send(row_send.at[k, other], row_recv.at[k, c], base + 5, device))

    def total(ref, n):
        terms = [ref[i].astype(F32) for i in range(n)]
        while len(terms) > 1:
            terms = [a + b for a, b in zip(terms[::2], terms[1::2], strict=True)]
        return terms[0]

    def split(both):
        return jnp.where(zh == 0, both[:16], both[16:]), jnp.where(zh == 0, both[16:], both[:16])

    def column_sums(k):
        base = 8 * k
        arrived(base + 4, col_recv.at[k, pl.ds(0, 15)])
        mine, theirs = split(total(col_recv.at[k], 16))
        part_send[k] = theirs
        send(part_send.at[k], part_recv.at[k], base + 6, partner)
        return mine, theirs

    def finish(k, mine):
        base = 8 * k
        arrived(base + 5, row_recv.at[k, pl.ds(0, 15)])
        out = mine + total(row_recv.at[k], 16)
        arrived(base + 6, part_recv.at[k])
        return out + part_recv[k]

    send_gather(0)
    send(xv, partner_x, 16, partner)
    for i in (1, 2, 3):
        loads[i].wait()
    sub = lax.broadcasted_iota(jnp.int32, (16, SLOTS), 0)
    lane = lax.broadcasted_iota(jnp.int32, (16, SLOTS), 1)
    alive = jnp.where(lane < count_s[0, 0], 1.0, 0.0)
    table = jnp.where(
        sub == 0, rows_v[0].astype(F32), jnp.where(sub == 1, cols_v[0].astype(F32), alive)
    ).astype(BF16)
    spread = jnp.where(
        lax.div(lax.broadcasted_iota(jnp.int32, (SLOTS, SLOTS * 16), 1), 16)
        == lax.broadcasted_iota(jnp.int32, (SLOTS, SLOTS * 16), 0),
        1.0, 0.0,
    ).astype(BF16)
    wide = jnp.dot(table, spread, preferred_element_type=F32).astype(jnp.int32)
    row_id, col_id, on = wide[0:1], wide[1:2], wide[2:3]
    pos = lax.broadcasted_iota(jnp.int32, (1, SLOTS * 16), 1)
    vec = lax.rem(pos, 8)
    half = lax.rem(lax.div(pos, 8), 2)
    key_f = jnp.where((on == 1) & (lax.rem(col_id, 2) == half), row_id * 8 + vec, -1)
    key_b = jnp.where((on == 1) & (lax.rem(row_id, 2) == half), col_id * 8 + vec, -1)
    strip = lax.broadcasted_iota(jnp.int32, (16, SLOTS * 16), 0)

    def fill_f(i, carry):
        hot_f[pl.ds(pl.multiple_of(i * 16, 16), 16), :] = jnp.where(strip + i * 16 == key_f, 1.0, 0.0).astype(BF16)
        return carry

    def fill_b(i, carry):
        hot_b[pl.ds(pl.multiple_of(i * 16, 16), 16), :] = jnp.where(strip + i * 16 == key_b, 1.0, 0.0).astype(BF16)
        return carry

    lax.fori_loop(0, 16, fill_f, 0)
    lax.fori_loop(0, 32, fill_b, 0)
    for i in (4, 5, 6, 8):
        loads[i].wait()

    loads[7].wait()
    rowp[c] = fold(pv[...]).astype(BF16)
    stack[0:8] = xv[...]
    stack[16:24] = pv[...]
    images[24:32] = hpv[...]
    transposed_part(0)
    forward_partner(0)
    send(pv, partner_p, 24, partner)
    each_line(lambda other, device: send(rowp.at[c], rowp.at[c], 25, device))
    mine, theirs = column_sums(0)

    arrived(16, partner_x)
    weighted = x_tall * mine + fold(partner_x[...]) * theirs
    squared = x_tall * x_tall
    num = jnp.sum(weighted[:8] + weighted[8:], axis=1, keepdims=True)
    den = jnp.sum(squared[:8] + squared[8:], axis=1, keepdims=True)
    sub8 = lax.broadcasted_iota(jnp.int32, (8, 128), 0)
    lane8 = lax.broadcasted_iota(jnp.int32, (8, 128), 1)
    placed = jnp.where(lane8 == sub8, num, jnp.where(lane8 == sub8 + 8, den, 0.0))
    th1[spot] = jnp.sum(placed, axis=0, keepdims=True)
    each_disc(lambda other, device: send(th1.at[spot], th1.at[spot], 17, device))
    forward_part(0)
    arrived(17, th1.at[pl.ds(0, 31)])
    acc = total(th1, 32)
    th2[z] = acc
    each_pole(lambda device: send(th2.at[z], th2.at[z], 18, device))

    arrived(25, rowp.at[pl.ds(0, 15)])
    paired_products(rowp)
    to_columns(colp_send, colp_recv, 26)

    hx_tall = finish(0, mine)
    arrived(18, th2.at[pl.ds(0, 15)])
    acc = total(th2, 16)
    num = 2.0 * jnp.sum(jnp.where(lane8 == sub8, acc, 0.0), axis=1, keepdims=True)
    den = jnp.sum(jnp.where(lane8 == sub8 + 8, acc, 0.0), axis=1, keepdims=True)
    theta = num / den
    theta_tall = jnp.concatenate([theta, theta], axis=0)
    res_tall = hx_tall - theta_tall * x_tall
    res_round = res_tall.astype(BF16)
    rowx[1][c] = res_round
    colx[1][r] = res_round

    send_gather(1)
    residual = unfold(res_tall)
    res_out[...] = residual
    stack[8:16] = residual
    stack[24:32] = unfold(hx_tall)
    images[0:24] = stack[0:24]
    images[32:40] = stack[24:32]
    images[40:48] = unfold(res_round.astype(F32))
    early = exact(stack[...], images[...])
    early = jnp.concatenate([early, jnp.zeros((32, 80), F32)], axis=1)
    for i in range(32):
        early_send[i] = early[i : i + 1]
    early1[spot] = early_send[spot]
    each_disc(lambda other, device: send(early_send.at[other], early1.at[spot], 19, device))
    arrived(26, colp_recv.at[pl.ds(0, 15)])
    arrived(24, partner_p)
    p_pair = jnp.concatenate([pv[...], partner_p[...]], axis=1)
    p_high = p_pair.astype(BF16).astype(F32)
    hp_mine, hp_theirs = split(total(colp_recv, 16))
    hp_pair = jnp.concatenate([unfold(hp_mine), unfold(hp_theirs)], axis=1)
    hp_high = hp_pair.astype(BF16)
    hp_low = (hp_pair - hp_high.astype(F32)).astype(BF16)
    transposed_part(1)
    forward_partner(1)
    arrived(19, early1.at[pl.ds(0, 31)])
    acc = total(early1, 32)
    early2[z] = acc
    each_pole(lambda device: send(early2.at[z], early2.at[z], 20, device))

    res_pair = jnp.concatenate([unfold(res_round.astype(F32)), unfold(colx[1][mate].astype(F32))], axis=1)
    res_pair = res_pair.astype(BF16)
    other_side = jnp.concatenate(
        [
            jnp.zeros((8, 8), F32),
            lax.dot_general(hp_high, res_pair, NT, preferred_element_type=F32)
            + lax.dot_general(hp_low, res_pair, NT, preferred_element_type=F32),
        ],
        axis=0,
    )
    sides = jnp.concatenate([res_pair.astype(F32), p_high, p_pair - p_high], axis=0).astype(BF16)
    mine, theirs = column_sums(1)
    pair = jnp.concatenate([unfold(mine), unfold(theirs)], axis=1)
    high = pair.astype(BF16)
    low = (pair - high.astype(F32)).astype(BF16)
    late = lax.dot_general(sides, high, NT, preferred_element_type=F32)
    late = late + lax.dot_general(sides, low, NT, preferred_element_type=F32)
    late = late[0:16] + jnp.concatenate([jnp.zeros((8, 8), F32), late[16:24]], axis=0) + other_side
    late = jnp.concatenate([late, jnp.zeros((16, 120), F32)], axis=1)
    late1[spot] = jnp.sum(pltpu.roll(late, 0, 1, stride=8, stride_axis=0), axis=0, keepdims=True)
    each_disc(lambda other, device: send(late1.at[spot], late1.at[spot], 22, device))
    forward_part(1)

    arrived(22, late1.at[pl.ds(0, 31)])
    late2[z] = total(late1, 32)
    each_pole(lambda device: send(late2.at[z], late2.at[z], 23, device))
    arrived(20, early2.at[pl.ds(0, 15)])
    early3[spot] = total(early2, 16)
    each_disc(lambda other, device: send(early3.at[spot], early3.at[spot], 21, device))

    img_out[...] = unfold(finish(1, mine))
    cells = 1.0 / 131072.0
    from_lane = lax.broadcasted_iota(jnp.int32, (128, 256), 1)
    from_vec = jnp.where(from_lane < 128, lax.rem(from_lane, 8), lax.div(from_lane - 128, 8))
    place = jnp.where(lax.broadcasted_iota(jnp.int32, (128, 256), 0) == 8 + from_vec, 1.0, 0.0)
    at = lax.broadcasted_iota(jnp.int32, (16, 256), 1)
    at_row = lax.broadcasted_iota(jnp.int32, (16, 256), 0)
    source = jnp.where(at < 128, lax.div(at, 8), jnp.where((at < 192) & (at_row < 8), lax.rem(at, 8), -1))
    arrived(21, early3.at[pl.ds(0, 31)])
    early = jnp.concatenate([early3[i] for i in range(32)], axis=0) * cells
    gs_out[...] = early[:24, :24]
    hx_part = pltpu.roll(early[:24], 128 - 32, 1)
    hp_part = pltpu.roll(early[:24], 128 - 8, 1)
    image_x = pltpu.roll(early[24:32], 128 - 32, 1)

    for which, ref in sent:
        wait_on(send_sem.at[which], ref)
    arrived(23, late2.at[pl.ds(0, 15)])
    late = total(late2, 16) * cells
    parts, rest = [], late
    for _ in range(3):
        part = rest.astype(BF16).astype(F32)
        rest = rest - part
        parts.append(jnp.where(source == at_row, jnp.concatenate([part, part], axis=1), 0.0))
    late = lax.dot_general(
        jnp.concatenate(parts, axis=0).astype(BF16), place.astype(BF16), NT, preferred_element_type=F32
    )
    late = late[0:16] + late[16:32] + late[32:48]
    image_part = jnp.concatenate([image_x, late], axis=0)
    lane24 = lax.broadcasted_iota(jnp.int32, (24, 128), 1)
    whole = jnp.where(lane24 < 8, hx_part, jnp.where(lane24 < 16, image_part, hp_part))
    gh_out[...] = whole[:, :24]
    wait_on(send_sem.at[23], late2.at[pl.ds(0, 15)])


def deliver(a, b, c, d, out_a, out_b, out_c, out_d, sem):
    pairs = ((a, out_a), (b, out_b), (c, out_c), (d, out_d))
    copies = [pltpu.make_async_copy(src, dst, sem.at[i]) for i, (src, dst) in enumerate(pairs)]
    for copy in copies:
        copy.start()
    for copy in copies:
        copy.wait()


def solution(mesh):
    def body(x_block, p_block, hp_block, tile_rows, tile_cols, tile_count, tile_values):
        any_spec = pl.BlockSpec(memory_space=pl.ANY)
        hbm = pl.BlockSpec(memory_space=pltpu.HBM)
        vmem = pl.BlockSpec(memory_space=pltpu.VMEM)
        shapes = (
            jax.ShapeDtypeStruct((8, 256), F32),
            jax.ShapeDtypeStruct((8, 256), F32),
            jax.ShapeDtypeStruct((24, 24), F32),
            jax.ShapeDtypeStruct((24, 24), F32),
        )
        results = pl.pallas_call(
            kernel,
            out_shape=shapes,
            in_specs=[any_spec] * 7,
            out_specs=(vmem,) * 4,
            scratch_shapes=[
                pltpu.VMEM((8, 256), F32), pltpu.VMEM((8, 256), F32), pltpu.VMEM((8, 256), F32),
                pltpu.VMEM((1, 1, SLOTS), jnp.int32), pltpu.VMEM((1, 1, SLOTS), jnp.int32),
                pltpu.SMEM((1, 1, SLOTS), jnp.int32), pltpu.SMEM((1, 1, SLOTS), jnp.int32),
                pltpu.SMEM((1, 1), jnp.int32),
                pltpu.VMEM((1, 1, SLOTS, 128, 128), BF16),
                pltpu.VMEM((256, SLOTS * 16), BF16), pltpu.VMEM((512, SLOTS * 16), BF16),
                pltpu.VMEM((SLOTS * 16, 128), BF16),
                pltpu.VMEM((16, 16, 128), BF16), pltpu.VMEM((16, 16, 128), BF16),
                pltpu.VMEM((32, 16, 128), BF16), pltpu.VMEM((32, 16, 128), BF16),
                pltpu.VMEM((2, 16, 16, 128), BF16), pltpu.VMEM((2, 16, 16, 128), BF16),
                pltpu.VMEM((2, 16, 32, 128), BF16), pltpu.VMEM((2, 16, 32, 128), BF16),
                pltpu.VMEM((2, 16, 128), F32), pltpu.VMEM((2, 16, 128), F32),
                pltpu.VMEM((32, 256), F32), pltpu.VMEM((48, 256), F32),
                pltpu.VMEM((8, 256), F32), pltpu.VMEM((8, 256), F32),
                pltpu.VMEM((16, 16, 128), BF16), pltpu.VMEM((16, 32, 128), BF16), pltpu.VMEM((16, 32, 128), BF16),
                pltpu.VMEM((32, 1, 128), F32), pltpu.VMEM((16, 1, 128), F32),
                pltpu.VMEM((32, 1, 128), F32), pltpu.VMEM((32, 1, 128), F32),
                pltpu.VMEM((16, 1, 128), F32), pltpu.VMEM((32, 1, 128), F32),
                pltpu.VMEM((32, 1, 128), F32), pltpu.VMEM((16, 1, 128), F32),
                pltpu.SemaphoreType.DMA((9,)), pltpu.SemaphoreType.DMA((27,)), pltpu.SemaphoreType.DMA((27,)),
            ],
            compiler_params=pltpu.CompilerParams(
                collective_id=0, has_side_effects=True, vmem_limit_bytes=VMEM_LIMIT
            ),
        )(*[pltpu.with_memory_space_constraint(v, pltpu.HBM) for v in (x_block, p_block, hp_block, tile_rows, tile_cols)], tile_count, pltpu.with_memory_space_constraint(tile_values, pltpu.HBM))
        return pl.pallas_call(
            deliver,
            out_shape=shapes,
            in_specs=[any_spec] * 4,
            out_specs=(any_spec,) * 4,
            scratch_shapes=[pltpu.SemaphoreType.DMA((4,))],
        )(*[pltpu.with_memory_space_constraint(v, pltpu.VMEM) for v in results])

    in_specs = (
        P(None, ("row", "col")),
        P(None, ("row", "col")),
        P(None, ("row", "col")),
        P("row", "col", None),
        P("row", "col", None),
        P("row", "col"),
        P("row", "col", None, None, None),
    )
    out_specs = (P(None, ("row", "col")), P(None, ("row", "col")), P(), P())
    return jax.shard_map(body, mesh=mesh, in_specs=in_specs, out_specs=out_specs, check_vma=False)
```
